32 devices in a mesh: ctx: 8 (over y, x, core), ulys: 4 (over z).
Axes of the slice: x: 2, y: 2, z: 4, core: 2. Of those that a mesh axis runs over, the one named last changes fastest.
Arguments:
- queries: bfloat16 [8192, 2048], P(('ctx', 'ulys')), may hold values from -32 to 32
- keys: bfloat16 [8192, 2048], P(('ctx', 'ulys')), may hold values from -32 to 32
- values: bfloat16 [8192, 2048], P(('ctx', 'ulys')), may hold values from -6 to 6
- rand_blocks: int32 [128, 3], replicated, may hold values from 0 to 127, as said below
- out_weight: bfloat16 [2048, 4096], replicated, may hold values from -0.125 to 0.125
Outputs:
- output: bfloat16 [8192, 4096], P(('ctx', 'ulys'))
The draws below stay inside these ranges and needn't reach their ends.
Inputs may be any that keep to these rules, and one draw needn't show every extreme that they name: `rand_blocks`: for the query blocks of one context group (rows 16 * c to 16 * c + 15), at most 12 of their random entries name blocks of any one group (blocks 16 * e to 16 * e + 15); every group's query blocks reach 12 for some group e.
All inputs are finite; a program needn't handle non-finite values.
Results may differ from the reference program's by a relative error of at most 0.0057.
Values may be sent and summed in bfloat16 or wider, within the bound.
No kernel may reach another device: no remote copies, remote signals or barrier semaphores. Data moves between devices by JAX's collectives and lax.ppermute only.
A program may use at most 192 MiB of HBM per device.

```python
import jax
import jax.numpy as jnp
from jax import lax

H = 16
DH = 128
D = 4096
BLK = 64
GLOB = 2
RAND = 3
TOKENS = 8192
QBG = 16
NB = 128
CAP = 12


def draw_queries(key, part):
    own_key = jax.random.fold_in(key, 11)
    filled = jnp.clip(jax.random.normal(own_key, (TOKENS, H * DH), jnp.float32), -6.0, 6.0)
    return filled.astype(jnp.bfloat16)


def draw_keys(key, part):
    own_key = jax.random.fold_in(key, 13)
    filled = jnp.clip(jax.random.normal(own_key, (TOKENS, H * DH), jnp.float32), -6.0, 6.0)
    return filled.astype(jnp.bfloat16)


def draw_rand_blocks(key, part):
    group_total = NB // QBG
    share = CAP // 2
    pair_count = max((group_total - 2) // 2, 1)
    slot_total = group_total * share

    def one_reader(reader_key):
        perm_key, split_key, within_key, order_key = jax.random.split(reader_key, 4)
        owners_perm = jax.random.permutation(perm_key, group_total).astype(jnp.int32)
        splits = jax.random.randint(split_key, (pair_count,), 0, 2 * share + 1, dtype=jnp.int32)
        slots = jnp.arange(slot_total, dtype=jnp.int32)
        shifted = slots - 2 * share
        pair_idx = jnp.clip(shifted // (2 * share), 0, pair_count - 1)
        within_pair = shifted % (2 * share)
        rank = jnp.where(slots < 2 * share, 0, jnp.where(within_pair < splits[pair_idx], 1 + 2 * pair_idx, 2 + 2 * pair_idx))
        owner = owners_perm[rank]
        within = jax.random.randint(within_key, (slot_total,), 0, QBG, dtype=jnp.int32)
        blocks = owner * QBG + within
        order = jax.random.permutation(order_key, slot_total)
        return blocks[order].reshape(QBG, RAND)
    reader_keys = jax.random.split(jax.random.fold_in(key, 17), group_total)
    return jax.vmap(one_reader)(reader_keys).reshape(NB, RAND).astype(jnp.int32)


def block_levels(stream_key, shape, cuts, low, high):
    def one(dim, shards_of):
        steps = jax.random.uniform(jax.random.fold_in(jax.random.fold_in(stream_key, 6), dim), (shards_of,), jnp.float32, low / len(cuts), high / len(cuts))
        return jnp.repeat(jnp.exp(steps), shape[dim] // shards_of).reshape((-1,) + (1,) * (len(shape) - dim - 1))

    loudness = one(*cuts[0])
    for cut in cuts[1:]:
        loudness = loudness * one(*cut)
    return loudness


def normal_values(key, shape, spread, reach, cuts=(), kind=jnp.bfloat16):
    drawn = jax.random.normal(key, shape, jnp.float32) * spread
    if len(cuts) > 0:
        drawn = block_levels(key, shape, cuts, -0.22, 0.18) * drawn
    return jnp.clip(drawn, min=-reach, max=reach).astype(kind)


def setup_inputs(seed: int = 0) -> dict:
    streams_of = jax.random.split(jax.random.key(seed), 6)
    return {
        "queries": draw_queries(jax.random.fold_in(streams_of[5], 71), 0),
        "keys": draw_keys(jax.random.fold_in(streams_of[5], 71), 0),
        "values": normal_values(streams_of[2], (TOKENS, H * DH), 1.0, 6.0, ((0, 32),)),
        "rand_blocks": draw_rand_blocks(jax.random.fold_in(streams_of[5], 71), 0),
        "out_weight": normal_values(streams_of[4], (H * DH, D), (H * DH) ** -0.5, 0.125),
    }


def reference(queries, keys, values, rand_blocks, out_weight):
    block_ids = jnp.arange(NB, dtype=jnp.int32)
    window = jnp.stack([(block_ids - 1) % NB, block_ids, (block_ids + 1) % NB], axis=1)
    leading = jnp.broadcast_to(jnp.arange(GLOB, dtype=jnp.int32)[None, :], (NB, GLOB))
    table = jnp.concatenate([window, leading, rand_blocks.astype(jnp.int32)], axis=1)
    query_blocks = queries.reshape(NB, BLK, H, DH)
    key_blocks = keys.reshape(NB, BLK, H, DH)
    value_blocks = values.reshape(NB, BLK, H, DH)
    group_count = NB // QBG

    def one_group(index):
        first = (index * QBG).astype(jnp.int32)
        rows = lax.dynamic_slice_in_dim(table, first, QBG, 0)
        query_grp = lax.dynamic_slice_in_dim(query_blocks, first, QBG, 0).astype(jnp.float32)
        key_grp = key_blocks[rows].reshape(QBG, -1, H, DH).astype(jnp.float32)
        value_grp = value_blocks[rows].reshape(QBG, -1, H, DH).astype(jnp.float32)
        scores = jnp.einsum("bqhd,bkhd->bhqk", query_grp, key_grp) * (DH ** -0.5)
        peak_score = jnp.max(scores, axis=-1, keepdims=True)
        lifted = jnp.exp(scores - peak_score)
        weights = (lifted / jnp.sum(lifted, axis=-1, keepdims=True)).astype(jnp.bfloat16)
        weights = lax.optimization_barrier(weights).astype(jnp.float32)
        attended = jnp.einsum("bhqk,bkhd->bqhd", weights, value_grp).astype(jnp.bfloat16)
        return attended.reshape(QBG * BLK, H * DH)

    attended = lax.map(one_group, jnp.arange(group_count, dtype=jnp.int32)).reshape(TOKENS, H * DH)
    return jnp.dot(attended, out_weight, preferred_element_type=jnp.float32).astype(jnp.bfloat16)
```

```python
import functools

import jax
import jax.numpy as jnp
from jax import lax
from jax.experimental import pallas as pl
from jax.experimental.pallas import tpu as pltpu
from jax.sharding import PartitionSpec as P

DH = 128
BLK = 64
GLOB = 2
RAND = 3
MIB = 1 << 20

ANY = pl.BlockSpec(memory_space=pl.ANY)
SMEM = pl.BlockSpec(memory_space=pltpu.SMEM)
VMEM = pl.BlockSpec(memory_space=pltpu.VMEM)


def copy_all(pairs, sems):
    copies = [pltpu.make_async_copy(src, dst, sems.at[i]) for i, (src, dst) in enumerate(pairs)]
    for c in copies:
        c.start()
    for c in copies:
        c.wait()


def mover(plan, n_in, out_shapes, n_copies, name, n_bytes):
    def body(place, *refs):
        ins, outs, sems = refs[:n_in], refs[n_in:-1], refs[-1]
        copy_all(plan(place, ins, outs), sems)

    return pl.pallas_call(
        body,
        out_shape=[jax.ShapeDtypeStruct(s, jnp.bfloat16) for s in out_shapes],
        in_specs=[SMEM] + [ANY] * n_in,
        out_specs=[ANY] * len(out_shapes),
        scratch_shapes=[pltpu.SemaphoreType.DMA((n_copies,))],
        cost_estimate=pl.CostEstimate(flops=0, bytes_accessed=2 * n_bytes, transcendentals=0),
        name=name,
    )


def pack(place, tensors, slots, n_u, hp):
    T = tensors[0].shape[0]
    nb = len(tensors)

    def plan(place, ins, outs):
        z, core = place[0], place[1]
        pairs = []
        for d in range(n_u):
            zd = lax.rem(z + d, n_u)
            for r in range(2):
                cr = core if r == 0 else 1 - core
                for i in range(nb):
                    col = ((2 * zd + cr) * hp + slots[i]) * DH
                    pairs.append((ins[i].at[:, pl.ds(pl.multiple_of(col, DH), DH)], outs[d].at[r, i]))
        return pairs

    call = mover(plan, nb, [(2, nb, T, DH)] * n_u, n_u * 2 * nb, "pack", 2 * n_u * nb * T * DH * 2)
    return call(place, *tensors)


def merge_other(place, parts):
    n_u = len(parts)
    _, nb, T, _ = parts[0].shape

    def plan(place, ins, outs):
        return [(ins[d].at[1], outs[0].at[d]) for d in range(n_u)]

    call = mover(plan, n_u, [(n_u, nb, T, DH)], n_u, "merge_other", n_u * nb * T * DH * 2)
    return call(place, *parts)[0]


def merge_own(place, parts, other):
    n_u = len(parts)
    _, nb, T, _ = parts[0].shape

    def plan(place, ins, outs):
        pairs = []
        for i in range(nb):
            for d in range(n_u):
                pairs.append((ins[d].at[0, i], outs[0].at[i, 0, d]))
                pairs.append((ins[n_u].at[d, i], outs[0].at[i, 1, d]))
        return pairs

    call = mover(
        plan, n_u + 1, [(nb, 2, n_u, T, DH)], 2 * nb * n_u, "merge_own", 2 * nb * n_u * T * DH * 2
    )
    return call(place, *parts, other)[0]


def shift(x, d, n_u):
    return lax.ppermute(x, "ulys", [(i, (i + d) % n_u) for i in range(n_u)])


def swap_core(x, n_c):
    return lax.ppermute(x, "ctx", [(i, i ^ 1) for i in range(n_c)])


def swap_chip(x, bit, n_c):
    return lax.ppermute(x, "ctx", [(i, i ^ (2 * bit)) for i in range(n_c)])


def to_heads(place, tensors, slots, n_u, n_c, hp):
    parts = pack(place, tensors, slots, n_u, hp)
    parts = [parts[0]] + [shift(parts[d], d, n_u) for d in range(1, n_u)]
    other = swap_core(merge_other(place, parts), n_c)
    return parts, other


def gather_chips(mine, n_c):
    rows = mine.shape[0]
    half = rows // 2
    n_p = n_c // 2
    halves = {0: (mine, None)}
    held = {0: [(mine, 0)]}
    for t in range(1, n_p):
        if t & (t - 1) == 0:
            got = swap_chip(mine, t, n_c)
            held[t] = [(got, 0)]
            halves[t] = (got[:half], got[half:])
    for t in range(1, n_p):
        if t & (t - 1) != 0:
            low = t & -t
            high = 1 << (t.bit_length() - 1)
            a = swap_chip(halves[t ^ low][0], low, n_c)
            b = swap_chip(halves[t ^ high][1], high, n_c)
            halves[t] = (a, b)
            held[t] = [(a, 0), (b, half)]
    return held


def pieces_of(held, index, count):
    rows = sum(a.shape[0] for a, _ in held[0])
    span = rows // count
    lo, hi = index * span, (index + 1) * span
    out = []
    for t in sorted(held):
        for a, first in held[t]:
            s, e = max(lo, first), min(hi, first + a.shape[0])
            if s < e:
                out.append((a, s - first, t * span + s - lo, e - s))
    return out


def attend(table, q_parts, q_other, q_index, k_pieces, v_pieces, n_u):
    T = q_parts[0].shape[2]
    n_q = 2 * n_u * T
    n_k = sum(p[3] for p in k_pieces)
    n_rows, n_list = table.shape
    group = T // BLK

    arrays = []

    def place_of(a):
        for i, b in enumerate(arrays):
            if a is b:
                return i
        arrays.append(a)
        return len(arrays) - 1

    q_at = [place_of(a) for a in q_parts] + [place_of(q_other)]
    k_at = [place_of(p[0]) for p in k_pieces]
    v_at = [place_of(p[0]) for p in v_pieces]
    n_in = len(arrays)
    n_copies = 2 * n_u + len(k_pieces) + len(v_pieces)

    def body(table, *refs):
        ins, outs = refs[:n_in], refs[n_in : n_in + n_u]
        q_vm, k_vm, v_vm, o_vm, sems, out_sems = refs[n_in + n_u :]
        pairs = []
        for d in range(n_u):
            pairs.append((ins[q_at[d]].at[0, q_index], q_vm.at[pl.ds(d * T, T)]))
            pairs.append((ins[q_at[n_u]].at[d, q_index], q_vm.at[pl.ds((n_u + d) * T, T)]))
        for at, pieces, vm in ((k_at, k_pieces, k_vm), (v_at, v_pieces, v_vm)):
            for i, (_, src, dst, n) in zip(at, pieces):
                pairs.append((ins[i].at[pl.ds(src, n)], vm.at[pl.ds(dst, n)]))
        copy_all(pairs, sems)

        @pl.loop(0, n_rows // group)
        def _(step):
            for g in range(group):
                row = step * group + g
                at = [pl.multiple_of(table[row, j] * BLK, BLK) for j in range(n_list)]
                q = q_vm[pl.ds(pl.multiple_of(row * BLK, BLK), BLK), :]
                k = jnp.concatenate([k_vm[pl.ds(a, BLK), :] for a in at], axis=0)
                v = jnp.concatenate([v_vm[pl.ds(a, BLK), :] for a in at], axis=0)
                s = lax.dot_general(
                    q, k, (((1,), (1,)), ((), ())), preferred_element_type=jnp.float32
                ) * (DH**-0.5)
                e = jnp.exp(s - jnp.max(s, axis=-1, keepdims=True))
                w = (e / jnp.sum(e, axis=-1, keepdims=True)).astype(jnp.bfloat16)
                o = jnp.dot(w, v, preferred_element_type=jnp.float32)
                o_vm[pl.ds(pl.multiple_of(row * BLK, BLK), BLK), :] = o.astype(jnp.bfloat16)

        copy_all(
            [
                (o_vm.at[pl.ds((r * n_u + d) * T, T)], outs[d].at[r, 0])
                for d in range(n_u)
                for r in range(2)
            ],
            out_sems,
        )

    flops = 4 * n_q * n_list * BLK * DH
    return pl.pallas_call(
        body,
        out_shape=[jax.ShapeDtypeStruct((2, 1, T, DH), jnp.bfloat16)] * n_u,
        in_specs=[SMEM] + [ANY] * n_in,
        out_specs=[ANY] * n_u,
        scratch_shapes=[
            pltpu.VMEM((n_q, DH), jnp.bfloat16),
            pltpu.VMEM((n_k, DH), jnp.bfloat16),
            pltpu.VMEM((n_k, DH), jnp.bfloat16),
            pltpu.VMEM((n_q, DH), jnp.bfloat16),
            pltpu.SemaphoreType.DMA((n_copies,)),
            pltpu.SemaphoreType.DMA((2 * n_u,)),
        ],
        compiler_params=pltpu.CompilerParams(
            vmem_limit_bytes=4 * (n_q + n_k) * DH + 8 * MIB
        ),
        cost_estimate=pl.CostEstimate(
            flops=flops, bytes_accessed=4 * (n_q + n_k) * DH, transcendentals=n_q * n_list * BLK
        ),
        name="attend",
    )(table, *arrays)


def project(place, own, other, weight, n_u, hp):
    T = own[0][0].shape[2]
    depth, width = weight.shape
    tile = 512
    arrays = [a for h in range(hp) for a in own[h]] + list(other)
    n_copies = 2 * hp * n_u

    def body(place, *refs):
        ins, w_ref, out_ref, rows, sems = refs[: len(arrays)], *refs[len(arrays) :]

        @pl.when(pl.program_id(0) == 0)
        def _():
            z, core = place[0], place[1]
            pairs = []
            for h in range(hp):
                for d in range(n_u):
                    zd = lax.rem(z + d, n_u)
                    for r in range(2):
                        cr = core if r == 0 else 1 - core
                        col = pl.multiple_of(((2 * zd + cr) * hp + h) * DH, DH)
                        src = ins[h * n_u + d].at[0, 0] if r == 0 else ins[hp * n_u + h].at[d, 0]
                        pairs.append((src, rows.at[:, pl.ds(col, DH)]))
            copy_all(pairs, sems)

        out_ref[...] = jnp.dot(
            rows[...], w_ref[...], preferred_element_type=jnp.float32
        ).astype(jnp.bfloat16)

    return pl.pallas_call(
        body,
        out_shape=jax.ShapeDtypeStruct((T, width), jnp.bfloat16),
        grid=(width // tile,),
        in_specs=[SMEM] + [ANY] * len(arrays) + [pl.BlockSpec((depth, tile), lambda j: (0, j))],
        out_specs=pl.BlockSpec((T, tile), lambda j: (0, j)),
        scratch_shapes=[
            pltpu.VMEM((T, depth), jnp.bfloat16),
            pltpu.SemaphoreType.DMA((n_copies,)),
        ],
        compiler_params=pltpu.CompilerParams(vmem_limit_bytes=16 * MIB),
        cost_estimate=pl.CostEstimate(
            flops=2 * T * depth * width,
            bytes_accessed=2 * (depth * width + T * (depth + width)),
            transcendentals=0,
        ),
        name="project",
    )(place, *arrays, weight)


def key_table(rand_blocks, z, core, chip, n_u, n_p, per):
    total = rand_blocks.shape[0]
    r = jnp.arange(2, dtype=jnp.int32)[:, None, None]
    d = jnp.arange(n_u, dtype=jnp.int32)[None, :, None]
    j = jnp.arange(per, dtype=jnp.int32)[None, None, :]
    mine = ((2 * chip + (core ^ r)) * n_u + (z - d) % n_u) * per + j
    mine = mine.reshape(-1)
    window = jnp.stack([(mine - 1) % total, mine, (mine + 1) % total], axis=1)
    leading = jnp.broadcast_to(jnp.arange(GLOB, dtype=jnp.int32)[None, :], (mine.shape[0], GLOB))
    listed = jnp.concatenate([window, leading, rand_blocks[mine]], axis=1)
    device, inner = listed // per, listed % per
    zs, cs = device % n_u, device // n_u
    mask, rel, shifted = (cs // 2) ^ chip, (cs % 2) ^ core, (z - zs) % n_u
    return ((mask * 2 + rel) * n_u + shifted) * per + inner


def shards(queries, keys, values, rand_blocks, out_weight):
    n_c, n_u = lax.axis_size("ctx"), lax.axis_size("ulys")
    T, lanes = queries.shape
    hp = lanes // DH // (2 * n_u)
    c, z = lax.axis_index("ctx"), lax.axis_index("ulys")
    chip, core = c // 2, c % 2
    place = jnp.stack([z, core]).astype(jnp.int32)
    table = key_table(rand_blocks, z, core, chip, n_u, n_c // 2, T // BLK)

    def spread(tensors, slots):
        parts, other = to_heads(place, tensors, slots, n_u, n_c, hp)
        held = gather_chips(merge_own(place, parts, other).reshape(-1, DH), n_c)
        return [pieces_of(held, i, len(tensors)) for i in range(len(tensors))]

    k_of, v_of = {}, {}
    (k_of[0],) = spread([keys], [0])
    (v_of[0],) = spread([values], [0])
    for h in range(1, hp):
        k_of[h], v_of[h] = spread([keys, values], [h, h])
    q_parts, q_other = to_heads(place, [queries] * hp, list(range(hp)), n_u, n_c, hp)

    own, other = [], []
    for h in range(hp):
        parts = attend(table, q_parts, q_other, h, k_of[h], v_of[h], n_u)
        parts = [parts[0]] + [shift(parts[d], n_u - d, n_u) for d in range(1, n_u)]
        own.append(parts)
        other.append(swap_core(merge_other(place, parts), n_c))
    return project(place, own, other, out_weight, n_u, hp)


def solution(mesh):
    return jax.shard_map(
        shards,
        mesh=mesh,
        in_specs=(
            P(("ctx", "ulys"), None),
            P(("ctx", "ulys"), None),
            P(("ctx", "ulys"), None),
            P(),
            P(),
        ),
        out_specs=P(("ctx", "ulys"), None),
        check_vma=False,
    )
```

```python
import functools

import jax
import jax.numpy as jnp
from jax import lax
from jax.experimental import pallas as pl
from jax.experimental.pallas import tpu as pltpu
from jax.sharding import PartitionSpec as P

DH = 128
BLK = 64
GLOB = 2
RAND = 3
MIB = 1 << 20
LOG2E = 1.4426950408889634

ANY = pl.BlockSpec(memory_space=pl.ANY)
SMEM = pl.BlockSpec(memory_space=pltpu.SMEM)
VMEM = pl.BlockSpec(memory_space=pltpu.VMEM)


WHOLE = pltpu.CompilerParams(vmem_limit_bytes=60 * MIB)


def cost(us):
    return pl.CostEstimate(flops=us * 1_150_000_000, bytes_accessed=0, transcendentals=0)


def copy_all(pairs, sems):
    copies = [pltpu.make_async_copy(src, dst, sems.at[i]) for i, (src, dst) in enumerate(pairs)]
    for c in copies:
        c.start()
    for c in copies:
        c.wait()


def sides(n_u):
    return [(r, d) for d in range(n_u) for r in range(2)]


def share_at(place, r, d, n_u):
    z, core = place[0], place[1]
    return 2 * lax.rem(z + d + n_u, n_u) + (core if r == 0 else 1 - core)


def stage(n_u, hp, here=None, tensors=(), slots=(), after=()):
    n_s = 2 * n_u
    ins = [x for x in (here,) if x is not None] + list(tensors)
    T = tensors[0].shape[0] if tensors else here.shape[2]
    n_split = 0 if here is None else here.shape[1]
    nb = len(tensors)
    n_copies = n_s * (n_split + nb)
    n_in = len(ins) + len(after)
    shapes = [(n_s * T, DH)] * n_split + [(n_s, nb, T, DH)] * (nb > 0)

    def body(*refs):
        outs, sems = refs[n_in:-1], refs[-1]
        pairs = []
        for k in range(n_s):
            for i in range(n_split):
                pairs.append((refs[0].at[k, i], outs[i].at[pl.ds(k * T, T)]))
            for i in range(nb):
                cols = pl.ds((k * hp + slots[i]) * DH, DH)
                pairs.append((refs[len(ins) - nb + i].at[:, cols], outs[-1].at[k, i]))
        copy_all(pairs, sems)

    return pl.pallas_call(
        body,
        out_shape=[jax.ShapeDtypeStruct(shape, jnp.bfloat16) for shape in shapes],
        in_specs=[ANY] * n_in,
        out_specs=[VMEM] * len(shapes),
        scratch_shapes=[pltpu.SemaphoreType.DMA((n_copies,))],
        compiler_params=WHOLE,
        cost_estimate=cost(3),
        name="stage",
    )(*ins, *after)


def to_shares(x, n_c, n_u):
    groups = [
        [(2 * p + core) * n_u + z for z in range(n_u) for core in range(2)] for p in range(n_c // 2)
    ]
    return lax.all_to_all(
        x, ("ctx", "ulys"), split_axis=0, concat_axis=0, tiled=True, axis_index_groups=groups
    )


def send(x, r, d, n_c, n_u):
    if (r, d) == (0, 0):
        return x
    pairs = [(c * n_u + z, (c ^ r) * n_u + (z + d) % n_u) for c in range(n_c) for z in range(n_u)]
    return lax.ppermute(x, ("ctx", "ulys"), pairs)


def send_all(parts, n_c, n_u, sign):
    return [send(x, r, (sign * d) % n_u, n_c, n_u) for x, (r, d) in zip(parts, sides(n_u))]


def swap_chip(x, bit, n_c):
    return lax.ppermute(x, "ctx", [(i, i ^ (2 * bit)) for i in range(n_c)])


def gather_chips(first, second, n_c):
    n_p = n_c // 2
    bits = [1 << i for i in range(n_p.bit_length() - 1)]
    a, b = {0: first}, {0: second}
    for t in reversed(bits):
        a[t] = swap_chip(first, t, n_c)
    for t in bits:
        b[t] = swap_chip(second, t, n_c)
    for t in range(1, n_p):
        if t not in bits:
            low, high = t & -t, 1 << (t.bit_length() - 1)
            a[t] = swap_chip(a[t ^ low], low, n_c)
            b[t] = swap_chip(b[t ^ high], high, n_c)
    return [a[t] for t in range(n_p)], [b[t] for t in range(n_p)]


def attend(place, table, queries, q_index, keys, values, n_u, apart, after):
    n_s, _, T, _ = queries.shape
    n_q = n_s * T
    span = keys[0].shape[0]
    n_k = span * len(keys)
    n_rows, n_list = table.shape
    group = 2 * T // BLK
    arrays = [queries, *keys, *values]
    n_in, n_out = len(arrays), 2 * n_u if apart else 1
    n_refs = n_in + len(after)

    def body(place, table, *refs):
        ins, outs = refs[:n_in], refs[n_refs : n_refs + n_out]
        q_vm, k_vm, v_vm, o_vm, sems, out_sems = refs[n_refs + n_out :]
        pairs = []
        for k in range(n_s):
            pairs.append((ins[0].at[k, q_index], q_vm.at[pl.ds(k * T, T)]))
        for i, ref in enumerate(ins[1:]):
            vm, t = (k_vm, i) if i < len(keys) else (v_vm, i - len(keys))
            pairs.append((ref, vm.at[pl.ds(t * span, span)]))
        copy_all(pairs, sems)

        @pl.loop(0, n_rows // group)
        def _(step):
            rows = [step * group + g for g in range(group)]
            at = [[pl.multiple_of(table[r, j] * BLK, BLK) for j in range(n_list)] for r in rows]
            s = []
            for r, listed in zip(rows, at):
                q = q_vm[pl.ds(pl.multiple_of(r * BLK, BLK), BLK), :]
                k = jnp.concatenate([k_vm[pl.ds(a, BLK), :] for a in listed], axis=0)
                s.append(
                    lax.dot_general(
                        q, k, (((1,), (1,)), ((), ())), preferred_element_type=jnp.float32
                    )
                )
            s = jnp.concatenate(s, axis=0)
            e = jnp.exp2((s - jnp.max(s, axis=-1, keepdims=True)) * (DH**-0.5 * LOG2E))
            w = (e * (1.0 / jnp.sum(e, axis=-1, keepdims=True))).astype(jnp.bfloat16)
            o = []
            for g, listed in enumerate(at):
                v = jnp.concatenate([v_vm[pl.ds(a, BLK), :] for a in listed], axis=0)
                o.append(
                    jnp.dot(
                        w[g * BLK : (g + 1) * BLK], v, preferred_element_type=jnp.float32
                    ).astype(jnp.bfloat16)
                )
            o_vm[pl.ds(pl.multiple_of(step * 2 * T, 2 * T), 2 * T), :] = jnp.concatenate(o, axis=0)

        pairs = []
        if apart:
            for out, (r, d) in zip(outs, sides(n_u)):
                at = pl.multiple_of(share_at(place, r, -d, n_u) * T, T)
                pairs.append((o_vm.at[pl.ds(at, T)], out))
        else:
            for k in range(n_s):
                pairs.append((o_vm.at[pl.ds(k * T, T)], outs[0].at[k]))
        copy_all(pairs, out_sems)

    return pl.pallas_call(
        body,
        out_shape=[jax.ShapeDtypeStruct((T, DH) if apart else (n_s, T, DH), jnp.bfloat16)] * n_out,
        in_specs=[SMEM, SMEM] + [ANY] * n_refs,
        out_specs=[ANY] * n_out,
        scratch_shapes=[
            pltpu.VMEM((n_q, DH), jnp.bfloat16),
            pltpu.VMEM((n_k, DH), jnp.bfloat16),
            pltpu.VMEM((n_k, DH), jnp.bfloat16),
            pltpu.VMEM((n_q, DH), jnp.bfloat16),
            pltpu.SemaphoreType.DMA((n_s + n_in - 1,)),
            pltpu.SemaphoreType.DMA((n_s,)),
        ],
        compiler_params=WHOLE,
        cost_estimate=cost(8),
        name="attend",
    )(place, table, *arrays, *after)


def project(place, parts, slot, weight, n_u, hp, partial):
    apart, last, more = isinstance(parts, list), slot == hp - 1, partial is not None
    arrays = parts if apart else [parts]
    n_in = len(arrays)
    T = arrays[0].shape[-2]
    width = weight.shape[1]
    shares = 2 * n_u
    depth = shares * DH
    tile = width // 2
    n_tiles = width // tile
    kind = jnp.bfloat16 if last else jnp.float32

    def body(place, *refs):
        ins, w_ref = refs[:n_in], refs[n_in]
        out_ref, rows, w_vm, add_vm, out_vm, row_sems, w_sems, add_sems, out_sems = refs[-9:]
        put = []
        for i, (r, d) in enumerate(sides(n_u)):
            src, share = (ins[i], share_at(place, r, d, n_u)) if apart else (ins[0].at[i], i)
            cols = pl.ds(pl.multiple_of(share * DH, DH), DH)
            put.append(pltpu.make_async_copy(src, rows.at[:, cols], row_sems.at[i]))
        fetch = []
        for t in range(n_tiles):
            cols = pl.ds(t * tile, tile)
            fetch.append([])
            for k in range(shares):
                src = w_ref.at[pl.ds((k * hp + slot) * DH, DH), cols]
                dst = w_vm.at[pl.ds(k * DH, DH), cols]
                fetch[t].append(pltpu.make_async_copy(src, dst, w_sems.at[t, k]))
            if more:
                src = refs[n_in + 1].at[:, cols]
                fetch[t].append(pltpu.make_async_copy(src, add_vm.at[:, cols], add_sems.at[t]))
        for c in put + sum(fetch, []):
            c.start()
        for c in put:
            c.wait()
        send = []
        for t in range(n_tiles):
            cols = pl.ds(t * tile, tile)
            for c in fetch[t]:
                c.wait()
            total = jnp.dot(rows[...], w_vm[:, cols], preferred_element_type=jnp.float32)
            if more:
                total = total + add_vm[:, cols]
            out_vm[:, cols] = total.astype(kind)
            send.append(
                pltpu.make_async_copy(out_vm.at[:, cols], out_ref.at[:, cols], out_sems.at[t])
            )
            send[-1].start()
        for c in send:
            c.wait()

    return pl.pallas_call(
        body,
        out_shape=jax.ShapeDtypeStruct((T, width), kind),
        in_specs=[SMEM] + [ANY] * (n_in + 1 + more),
        out_specs=ANY,
        scratch_shapes=[
            pltpu.VMEM((T, depth), jnp.bfloat16),
            pltpu.VMEM((depth, width), jnp.bfloat16),
            pltpu.VMEM((T, width), jnp.float32),
            pltpu.VMEM((T, width), kind),
            pltpu.SemaphoreType.DMA((shares,)),
            pltpu.SemaphoreType.DMA((n_tiles, shares)),
            pltpu.SemaphoreType.DMA((n_tiles,)),
            pltpu.SemaphoreType.DMA((n_tiles,)),
        ],
        compiler_params=WHOLE,
        cost_estimate=cost(8),
        name="project",
    )(place, *arrays, weight, *([partial] * more))


def key_table(rand_blocks, chip, n_u, n_p, per):
    total = rand_blocks.shape[0]
    z = jnp.arange(n_u, dtype=jnp.int32)[:, None, None]
    core = jnp.arange(2, dtype=jnp.int32)[None, :, None]
    j = jnp.arange(per, dtype=jnp.int32)[None, None, :]
    mine = (((2 * chip + core) * n_u + z) * per + j).reshape(-1)
    window = jnp.stack([(mine - 1) % total, mine, (mine + 1) % total], axis=1)
    leading = jnp.broadcast_to(jnp.arange(GLOB, dtype=jnp.int32)[None, :], (mine.shape[0], GLOB))
    listed = jnp.concatenate([window, leading, rand_blocks[mine]], axis=1)
    device, inner = listed // per, listed % per
    zs, cs = device % n_u, device // n_u
    return ((((cs // 2) ^ chip) * n_u + zs) * 2 + cs % 2) * per + inner


def shards(queries, keys, values, rand_blocks, out_weight):
    n_c, n_u = lax.axis_size("ctx"), lax.axis_size("ulys")
    T, lanes = queries.shape
    hp = lanes // DH // (2 * n_u)
    c, z = lax.axis_index("ctx"), lax.axis_index("ulys")
    chip, core = c // 2, c % 2
    place = jnp.stack([z, core]).astype(jnp.int32)
    table = key_table(rand_blocks, chip, n_u, n_c // 2, T // BLK)

    kv, after = [], ()
    (packed,) = stage(n_u, hp, None, [keys, values], [0, 0])
    for h in range(hp):
        here = to_shares(packed, n_c, n_u)
        if h < hp - 1:
            tensors, slots = [keys, values], [h + 1, h + 1]
        else:
            tensors, slots = [queries] * hp, list(range(hp))
        first, second, packed = stage(n_u, hp, here, tensors, slots, (table, *after))
        kv.append(gather_chips(first, second, n_c))
        after = [side[1 << i] for side in kv[-1] for i in range((n_c // 2).bit_length() - 1)]
    q_here = to_shares(packed, n_c, n_u)

    total = None
    for h in range(hp):
        last = h == hp - 1
        parts = attend(place, table, q_here, h, *kv[h], n_u, last, after)
        parts = send_all(parts, n_c, n_u, -1) if last else to_shares(parts[0], n_c, n_u)
        total = project(place, parts, h, out_weight, n_u, hp, total)
    return total


def solution(mesh):
    return jax.shard_map(
        shards,
        mesh=mesh,
        in_specs=(
            P(("ctx", "ulys"), None),
            P(("ctx", "ulys"), None),
            P(("ctx", "ulys"), None),
            P(),
            P(),
        ),
        out_specs=P(("ctx", "ulys"), None),
        check_vma=False,
    )
```

```python
import functools

import jax
import jax.numpy as jnp
from jax import lax
from jax.experimental import pallas as pl
from jax.experimental.pallas import tpu as pltpu
from jax.sharding import PartitionSpec as P

DH = 128
BLK = 64
GLOB = 2
RAND = 3
MIB = 1 << 20
LOG2E = 1.4426950408889634

ANY = pl.BlockSpec(memory_space=pl.ANY)
SMEM = pl.BlockSpec(memory_space=pltpu.SMEM)
VMEM = pl.BlockSpec(memory_space=pltpu.VMEM)


WHOLE = pltpu.CompilerParams(vmem_limit_bytes=60 * MIB)


def cost(us):
    return pl.CostEstimate(flops=us * 1_150_000_000, bytes_accessed=0, transcendentals=0)


def copy_all(pairs, sems):
    copies = [pltpu.make_async_copy(src, dst, sems.at[i]) for i, (src, dst) in enumerate(pairs)]
    for c in copies:
        c.start()
    for c in copies:
        c.wait()


def sides(n_u):
    return [(r, d) for d in range(n_u) for r in range(2)]


def share_at(place, r, d, n_u):
    z, core = place[0], place[1]
    return 2 * lax.rem(z + d + n_u, n_u) + (core if r == 0 else 1 - core)


def pack_sides(place, tensors, slots, n_u, hp):
    T, nb, n_out = tensors[0].shape[0], len(tensors), 2 * n_u

    def body(place, *refs):
        ins, outs, sems = refs[:nb], refs[nb:-1], refs[-1]
        pairs = []
        for out, (r, d) in zip(outs, sides(n_u)):
            for i in range(nb):
                col = (share_at(place, r, d, n_u) * hp + slots[i]) * DH
                pairs.append((ins[i].at[:, pl.ds(pl.multiple_of(col, DH), DH)], out.at[i]))
        copy_all(pairs, sems)

    return pl.pallas_call(
        body,
        out_shape=[jax.ShapeDtypeStruct((nb, T, DH), jnp.bfloat16)] * n_out,
        in_specs=[SMEM] + [ANY] * nb,
        out_specs=[VMEM] * n_out,
        scratch_shapes=[pltpu.SemaphoreType.DMA((n_out * nb,))],
        compiler_params=WHOLE,
        cost_estimate=cost(3),
        name="pack_sides",
    )(place, *tensors)


def stage(place, here, tensors, slots, n_u, hp, after):
    apart = isinstance(here, list)
    blocks = here if apart else [here]
    n_s, n_b, nb = 2 * n_u, len(blocks), len(tensors)
    n_split, T = 2, blocks[0].shape[-2]
    n_copies = n_s * (n_split + nb)
    n_in = n_b + nb + len(after)
    shapes = [(n_s * T, DH)] * n_split + [(n_s, nb, T, DH)]

    def body(place, *refs):
        outs, sems = refs[n_in:-1], refs[-1]
        pairs = []
        for k, (r, d) in enumerate(sides(n_u)):
            block, sender = (refs[k], share_at(place, r, -d, n_u)) if apart else (refs[0].at[k], k)
            for i in range(n_split):
                pairs.append((block.at[i], outs[i].at[pl.ds(pl.multiple_of(sender * T, T), T)]))
            for i in range(nb):
                cols = pl.ds((k * hp + slots[i]) * DH, DH)
                pairs.append((refs[n_b + i].at[:, cols], outs[-1].at[k, i]))
        copy_all(pairs, sems)

    return pl.pallas_call(
        body,
        out_shape=[jax.ShapeDtypeStruct(shape, jnp.bfloat16) for shape in shapes],
        in_specs=[SMEM] + [ANY] * n_in,
        out_specs=[VMEM] * len(shapes),
        scratch_shapes=[pltpu.SemaphoreType.DMA((n_copies,))],
        compiler_params=WHOLE,
        cost_estimate=cost(3),
        name="stage",
    )(place, *blocks, *tensors, *after)


def to_shares(x, n_c, n_u):
    groups = [
        [(2 * p + core) * n_u + z for z in range(n_u) for core in range(2)] for p in range(n_c // 2)
    ]
    return lax.all_to_all(
        x, ("ctx", "ulys"), split_axis=0, concat_axis=0, tiled=True, axis_index_groups=groups
    )


def send(x, r, d, n_c, n_u):
    if (r, d) == (0, 0):
        return x
    pairs = [(c * n_u + z, (c ^ r) * n_u + (z + d) % n_u) for c in range(n_c) for z in range(n_u)]
    return lax.ppermute(x, ("ctx", "ulys"), pairs)


def send_all(parts, n_c, n_u, sign):
    return [send(x, r, (sign * d) % n_u, n_c, n_u) for x, (r, d) in zip(parts, sides(n_u))]


def swap_chip(x, bit, n_c):
    return lax.ppermute(x, "ctx", [(i, i ^ (2 * bit)) for i in range(n_c)])


def gather_chips(first, second, n_c):
    n_p = n_c // 2
    bits = [1 << i for i in range(n_p.bit_length() - 1)]
    a, b = {0: first}, {0: second}
    for t in reversed(bits):
        a[t] = swap_chip(first, t, n_c)
    for t in bits:
        b[t] = swap_chip(second, t, n_c)
    for t in range(1, n_p):
        if t not in bits:
            low, high = t & -t, 1 << (t.bit_length() - 1)
            a[t] = swap_chip(a[t ^ low], low, n_c)
            b[t] = swap_chip(b[t ^ high], high, n_c)
    return [a[t] for t in range(n_p)], [b[t] for t in range(n_p)]


def attend(place, table, queries, q_index, keys, values, n_u, apart, after):
    n_s, _, T, _ = queries.shape
    n_q = n_s * T
    span = keys[0].shape[0]
    n_k = span * len(keys)
    n_rows, n_list = table.shape
    group = 2 * T // BLK
    arrays = [queries, *keys, *values]
    n_in, n_out = len(arrays), 2 * n_u if apart else 1
    n_refs = n_in + len(after)

    def body(place, table, *refs):
        ins, outs = refs[:n_in], refs[n_refs : n_refs + n_out]
        q_vm, k_vm, v_vm, o_vm, sems, out_sems = refs[n_refs + n_out :]
        pairs = []
        for k in range(n_s):
            pairs.append((ins[0].at[k, q_index], q_vm.at[pl.ds(k * T, T)]))
        for i, ref in enumerate(ins[1:]):
            vm, t = (k_vm, i) if i < len(keys) else (v_vm, i - len(keys))
            pairs.append((ref, vm.at[pl.ds(t * span, span)]))
        copy_all(pairs, sems)

        @pl.loop(0, n_rows // group)
        def _(step):
            rows = [step * group + g for g in range(group)]
            at = [[pl.multiple_of(table[r, j] * BLK, BLK) for j in range(n_list)] for r in rows]
            s = []
            for r, listed in zip(rows, at):
                q = q_vm[pl.ds(pl.multiple_of(r * BLK, BLK), BLK), :]
                k = jnp.concatenate([k_vm[pl.ds(a, BLK), :] for a in listed], axis=0)
                s.append(
                    lax.dot_general(
                        q, k, (((1,), (1,)), ((), ())), preferred_element_type=jnp.float32
                    )
                )
            s = jnp.concatenate(s, axis=0)
            e = jnp.exp2((s - jnp.max(s, axis=-1, keepdims=True)) * (DH**-0.5 * LOG2E))
            w = (e * (1.0 / jnp.sum(e, axis=-1, keepdims=True))).astype(jnp.bfloat16)
            o = []
            for g, listed in enumerate(at):
                v = jnp.concatenate([v_vm[pl.ds(a, BLK), :] for a in listed], axis=0)
                o.append(
                    jnp.dot(
                        w[g * BLK : (g + 1) * BLK], v, preferred_element_type=jnp.float32
                    ).astype(jnp.bfloat16)
                )
            o_vm[pl.ds(pl.multiple_of(step * 2 * T, 2 * T), 2 * T), :] = jnp.concatenate(o, axis=0)

        pairs = []
        if apart:
            for out, (r, d) in zip(outs, sides(n_u)):
                at = pl.multiple_of(share_at(place, r, -d, n_u) * T, T)
                pairs.append((o_vm.at[pl.ds(at, T)], out))
        else:
            for k in range(n_s):
                pairs.append((o_vm.at[pl.ds(k * T, T)], outs[0].at[k]))
        copy_all(pairs, out_sems)

    return pl.pallas_call(
        body,
        out_shape=[jax.ShapeDtypeStruct((T, DH) if apart else (n_s, T, DH), jnp.bfloat16)] * n_out,
        in_specs=[SMEM, SMEM] + [ANY] * n_refs,
        out_specs=[ANY] * n_out,
        scratch_shapes=[
            pltpu.VMEM((n_q, DH), jnp.bfloat16),
            pltpu.VMEM((n_k, DH), jnp.bfloat16),
            pltpu.VMEM((n_k, DH), jnp.bfloat16),
            pltpu.VMEM((n_q, DH), jnp.bfloat16),
            pltpu.SemaphoreType.DMA((n_s + n_in - 1,)),
            pltpu.SemaphoreType.DMA((n_s,)),
        ],
        compiler_params=WHOLE,
        cost_estimate=cost(8),
        name="attend",
    )(place, table, *arrays, *after)


def project(place, parts, slot, weight, n_u, hp, partial):
    apart, last, more = isinstance(parts, list), slot == hp - 1, partial is not None
    arrays = parts if apart else [parts]
    n_in = len(arrays)
    T = arrays[0].shape[-2]
    width = weight.shape[1]
    shares = 2 * n_u
    depth = shares * DH
    tile = width // 2
    n_tiles = width // tile
    kind = jnp.bfloat16 if last else jnp.float32

    def body(place, *refs):
        ins, w_ref = refs[:n_in], refs[n_in]
        out_ref, rows, w_vm, add_vm, out_vm, row_sems, w_sems, add_sems, out_sems = refs[-9:]
        put = []
        for i, (r, d) in enumerate(sides(n_u)):
            src, share = (ins[i], share_at(place, r, d, n_u)) if apart else (ins[0].at[i], i)
            cols = pl.ds(pl.multiple_of(share * DH, DH), DH)
            put.append(pltpu.make_async_copy(src, rows.at[:, cols], row_sems.at[i]))
        fetch = []
        for t in range(n_tiles):
            cols = pl.ds(t * tile, tile)
            fetch.append([])
            for k in range(shares):
                src = w_ref.at[pl.ds((k * hp + slot) * DH, DH), cols]
                dst = w_vm.at[pl.ds(k * DH, DH), cols]
                fetch[t].append(pltpu.make_async_copy(src, dst, w_sems.at[t, k]))
            if more:
                src = refs[n_in + 1].at[:, cols]
                fetch[t].append(pltpu.make_async_copy(src, add_vm.at[:, cols], add_sems.at[t]))
        for c in put + sum(fetch, []):
            c.start()
        for c in put:
            c.wait()
        send = []
        for t in range(n_tiles):
            cols = pl.ds(t * tile, tile)
            for c in fetch[t]:
                c.wait()
            total = jnp.dot(rows[...], w_vm[:, cols], preferred_element_type=jnp.float32)
            if more:
                total = total + add_vm[:, cols]
            out_vm[:, cols] = total.astype(kind)
            send.append(
                pltpu.make_async_copy(out_vm.at[:, cols], out_ref.at[:, cols], out_sems.at[t])
            )
            send[-1].start()
        for c in send:
            c.wait()

    return pl.pallas_call(
        body,
        out_shape=jax.ShapeDtypeStruct((T, width), kind),
        in_specs=[SMEM] + [ANY] * (n_in + 1 + more),
        out_specs=ANY,
        scratch_shapes=[
            pltpu.VMEM((T, depth), jnp.bfloat16),
            pltpu.VMEM((depth, width), jnp.bfloat16),
            pltpu.VMEM((T, width), jnp.float32),
            pltpu.VMEM((T, width), kind),
            pltpu.SemaphoreType.DMA((shares,)),
            pltpu.SemaphoreType.DMA((n_tiles, shares)),
            pltpu.SemaphoreType.DMA((n_tiles,)),
            pltpu.SemaphoreType.DMA((n_tiles,)),
        ],
        compiler_params=WHOLE,
        cost_estimate=cost(8),
        name="project",
    )(place, *arrays, weight, *([partial] * more))


def key_table(rand_blocks, chip, n_u, n_p, per):
    total = rand_blocks.shape[0]
    z = jnp.arange(n_u, dtype=jnp.int32)[:, None, None]
    core = jnp.arange(2, dtype=jnp.int32)[None, :, None]
    j = jnp.arange(per, dtype=jnp.int32)[None, None, :]
    mine = (((2 * chip + core) * n_u + z) * per + j).reshape(-1)
    window = jnp.stack([(mine - 1) % total, mine, (mine + 1) % total], axis=1)
    leading = jnp.broadcast_to(jnp.arange(GLOB, dtype=jnp.int32)[None, :], (mine.shape[0], GLOB))
    listed = jnp.concatenate([window, leading, rand_blocks[mine]], axis=1)
    device, inner = listed // per, listed % per
    zs, cs = device % n_u, device // n_u
    return ((((cs // 2) ^ chip) * n_u + zs) * 2 + cs % 2) * per + inner


def shards(queries, keys, values, rand_blocks, out_weight):
    n_c, n_u = lax.axis_size("ctx"), lax.axis_size("ulys")
    T, lanes = queries.shape
    hp = lanes // DH // (2 * n_u)
    c, z = lax.axis_index("ctx"), lax.axis_index("ulys")
    chip, core = c // 2, c % 2
    place = jnp.stack([z, core]).astype(jnp.int32)
    table = key_table(rand_blocks, chip, n_u, n_c // 2, T // BLK)

    q_of, kv, after = [], [], (table,)
    here = send_all(pack_sides(place, [keys, values], [0, 0], n_u, hp), n_c, n_u, 1)
    for h in range(hp):
        if h < hp - 1:
            tensors, slots = [keys, values, queries], [h + 1, h + 1, h]
        else:
            tensors, slots = [queries], [h]
        first, second, packed = stage(place, here, tensors, slots, n_u, hp, after)
        here = to_shares(packed, n_c, n_u)
        q_of.append((here, len(tensors) - 1))
        kv.append(gather_chips(first, second, n_c))
        after = [x for side in kv[-1] for x in side[1:]]

    total = None
    for h in range(hp):
        last = h == hp - 1
        parts = attend(place, table, *q_of[h], *kv[h], n_u, last, ())
        parts = send_all(parts, n_c, n_u, -1) if last else to_shares(parts[0], n_c, n_u)
        total = project(place, parts, h, out_weight, n_u, hp, total)
    return total


def solution(mesh):
    return jax.shard_map(
        shards,
        mesh=mesh,
        in_specs=(
            P(("ctx", "ulys"), None),
            P(("ctx", "ulys"), None),
            P(("ctx", "ulys"), None),
            P(),
            P(),
        ),
        out_specs=P(("ctx", "ulys"), None),
        check_vma=False,
    )
```

```python
import functools

import jax
import jax.numpy as jnp
from jax import lax
from jax.experimental import pallas as pl
from jax.experimental.pallas import tpu as pltpu
from jax.sharding import PartitionSpec as P

DH = 128
BLK = 64
GLOB = 2
RAND = 3
MIB = 1 << 20
LOG2E = 1.4426950408889634

ANY = pl.BlockSpec(memory_space=pl.ANY)
SMEM = pl.BlockSpec(memory_space=pltpu.SMEM)
VMEM = pl.BlockSpec(memory_space=pltpu.VMEM)


WHOLE = pltpu.CompilerParams(vmem_limit_bytes=60 * MIB)


def beside(n_bytes):
    return pltpu.CompilerParams(vmem_limit_bytes=60 * MIB - n_bytes)


def cost(us):
    return pl.CostEstimate(flops=us * 1_150_000_000, bytes_accessed=0, transcendentals=0)


def copy_all(pairs, sems):
    copies = [pltpu.make_async_copy(src, dst, sems.at[i]) for i, (src, dst) in enumerate(pairs)]
    for c in copies:
        c.start()
    for c in copies:
        c.wait()


def sides(n_u):
    return [(r, d) for d in range(n_u) for r in range(2)]


def share_at(place, r, d, n_u):
    z, core = place[0], place[1]
    return 2 * lax.rem(z + d + n_u, n_u) + (core if r == 0 else 1 - core)


def pack_sides(place, tensors, slots, n_u):
    T, nb, n_out = tensors[0].shape[0], len(tensors), 2 * n_u

    def body(place, *refs):
        ins, outs, sems = refs[:nb], refs[nb:-1], refs[-1]
        pairs = []
        for out, (r, d) in zip(outs, sides(n_u)):
            for i in range(nb):
                col = (slots[i] * n_out + share_at(place, r, d, n_u)) * DH
                pairs.append((ins[i].at[:, pl.ds(pl.multiple_of(col, DH), DH)], out.at[i]))
        copy_all(pairs, sems)

    return pl.pallas_call(
        body,
        out_shape=[jax.ShapeDtypeStruct((nb, T, DH), jnp.bfloat16)] * n_out,
        in_specs=[SMEM] + [ANY] * nb,
        out_specs=[VMEM] * n_out,
        scratch_shapes=[pltpu.SemaphoreType.DMA((n_out * nb,))],
        compiler_params=WHOLE,
        cost_estimate=cost(3),
        name="pack_sides",
    )(place, *tensors)


def stage(place, here, tensors, slots, n_u, after):
    apart = isinstance(here, list)
    blocks = here if apart else [here]
    n_s, n_b, nb = 2 * n_u, len(blocks), len(tensors)
    n_split, T = 2, blocks[0].shape[-2]
    n_copies = n_s * (n_split + nb)
    n_in = n_b + nb + len(after)
    shapes = [(n_s * T, DH)] * n_split + [(n_s, nb, T, DH)]

    def body(place, *refs):
        outs, sems = refs[n_in:-1], refs[-1]
        pairs = []
        for k, (r, d) in enumerate(sides(n_u)):
            block, sender = (refs[k], share_at(place, r, -d, n_u)) if apart else (refs[0].at[k], k)
            for i in range(n_split):
                pairs.append((block.at[i], outs[i].at[pl.ds(pl.multiple_of(sender * T, T), T)]))
            for i in range(nb):
                cols = pl.ds((slots[i] * n_s + k) * DH, DH)
                pairs.append((refs[n_b + i].at[:, cols], outs[-1].at[k, i]))
        copy_all(pairs, sems)

    return pl.pallas_call(
        body,
        out_shape=[jax.ShapeDtypeStruct(shape, jnp.bfloat16) for shape in shapes],
        in_specs=[SMEM] + [ANY] * n_in,
        out_specs=[VMEM] * len(shapes),
        scratch_shapes=[pltpu.SemaphoreType.DMA((n_copies,))],
        compiler_params=WHOLE,
        cost_estimate=cost(3),
        name="stage",
    )(place, *blocks, *tensors, *after)


def to_shares(x, n_c, n_u):
    groups = [
        [(2 * p + core) * n_u + z for z in range(n_u) for core in range(2)] for p in range(n_c // 2)
    ]
    return lax.all_to_all(
        x, ("ctx", "ulys"), split_axis=0, concat_axis=0, tiled=True, axis_index_groups=groups
    )


def send(x, r, d, n_c, n_u):
    if (r, d) == (0, 0):
        return x
    pairs = [(c * n_u + z, (c ^ r) * n_u + (z + d) % n_u) for c in range(n_c) for z in range(n_u)]
    return lax.ppermute(x, ("ctx", "ulys"), pairs)


def send_all(parts, n_c, n_u, sign):
    return [send(x, r, (sign * d) % n_u, n_c, n_u) for x, (r, d) in zip(parts, sides(n_u))]


def swap_chip(x, bit, n_c):
    return lax.ppermute(x, "ctx", [(i, i ^ (2 * bit)) for i in range(n_c)])


def gather_chips(first, second, n_c):
    n_p = n_c // 2
    bits = [1 << i for i in range(n_p.bit_length() - 1)]
    a, b = {0: first}, {0: second}
    for t in reversed(bits):
        a[t] = swap_chip(first, t, n_c)
    for t in bits:
        b[t] = swap_chip(second, t, n_c)
    for t in range(1, n_p):
        if t not in bits:
            low, high = t & -t, 1 << (t.bit_length() - 1)
            a[t] = swap_chip(a[t ^ low], low, n_c)
            b[t] = swap_chip(b[t ^ high], high, n_c)
    return [a[t] for t in range(n_p)], [b[t] for t in range(n_p)]


def attend(place, table, queries, q_index, keys, values, n_u, apart):
    n_s, _, T, _ = queries.shape
    n_q = n_s * T
    span = keys[0].shape[0]
    n_k = span * len(keys)
    n_rows, n_list = table.shape
    group = 4 * T // BLK
    arrays = [queries, *keys, *values]
    n_in, n_out = len(arrays), 2 * n_u if apart else 1

    def body(place, table, *refs):
        ins, outs = refs[:n_in], refs[n_in : n_in + n_out]
        q_vm, k_vm, v_vm, o_vm, sems, out_sems = refs[n_in + n_out :]
        pairs = []
        for k in range(n_s):
            pairs.append((ins[0].at[k, q_index], q_vm.at[pl.ds(k * T, T)]))
        for i, ref in enumerate(ins[1:]):
            vm, t = (k_vm, i) if i < len(keys) else (v_vm, i - len(keys))
            pairs.append((ref, vm.at[pl.ds(t * span, span)]))
        copies = [pltpu.make_async_copy(a, b, sems.at[i]) for i, (a, b) in enumerate(pairs)]
        for c in copies:
            c.start()
        for c in copies[: n_s + len(keys)]:
            c.wait()
        for step in range(n_rows // group):
            rows = range(step * group, (step + 1) * group)
            at = [[pl.multiple_of(table[r, j] * BLK, BLK) for j in range(n_list)] for r in rows]
            s = []
            for r, listed in zip(rows, at):
                k = jnp.concatenate([k_vm[pl.ds(a, BLK), :] for a in listed], axis=0)
                s.append(
                    lax.dot_general(
                        q_vm[pl.ds(r * BLK, BLK), :],
                        k,
                        (((1,), (1,)), ((), ())),
                        preferred_element_type=jnp.float32,
                    )
                )
            s = jnp.concatenate(s, axis=0)
            e = jnp.exp2((s - jnp.max(s, axis=-1, keepdims=True)) * (DH**-0.5 * LOG2E))
            w = (e * (1.0 / jnp.sum(e, axis=-1, keepdims=True))).astype(jnp.bfloat16)
            if step == 0:
                for c in copies[n_s + len(keys) :]:
                    c.wait()
            for g, (r, listed) in enumerate(zip(rows, at)):
                v = jnp.concatenate([v_vm[pl.ds(a, BLK), :] for a in listed], axis=0)
                o = jnp.dot(
                    w[g * BLK : (g + 1) * BLK], v, preferred_element_type=jnp.float32
                )
                o_vm[pl.ds(r * BLK, BLK), :] = o.astype(jnp.bfloat16)

        pairs = []
        if apart:
            for out, (r, d) in zip(outs, sides(n_u)):
                at = pl.multiple_of(share_at(place, r, -d, n_u) * T, T)
                pairs.append((o_vm.at[pl.ds(at, T)], out))
        else:
            for k in range(n_s):
                pairs.append((o_vm.at[pl.ds(k * T, T)], outs[0].at[k]))
        copy_all(pairs, out_sems)

    return pl.pallas_call(
        body,
        out_shape=[jax.ShapeDtypeStruct((T, DH) if apart else (n_s, T, DH), jnp.bfloat16)] * n_out,
        in_specs=[SMEM, SMEM] + [ANY] * n_in,
        out_specs=[ANY] * n_out,
        scratch_shapes=[
            pltpu.VMEM((n_q, DH), jnp.bfloat16),
            pltpu.VMEM((n_k, DH), jnp.bfloat16),
            pltpu.VMEM((n_k, DH), jnp.bfloat16),
            pltpu.VMEM((n_q, DH), jnp.bfloat16),
            pltpu.SemaphoreType.DMA((n_s + n_in - 1,)),
            pltpu.SemaphoreType.DMA((n_s,)),
        ],
        compiler_params=WHOLE,
        cost_estimate=cost(8),
        name="attend",
    )(place, table, *arrays)


def project(place, parts, weight, slot, n_u, hp, partial):
    apart, last = isinstance(parts, list), slot == hp - 1
    arrays = parts if apart else [parts]
    T = arrays[0].shape[-2]
    width = weight.shape[1]
    shares = 2 * n_u
    depth = shares * DH
    n_tiles, n_chunks = 2, 1
    tile, chunk = width // n_tiles, depth // n_chunks
    n_in = len(arrays)
    kept = [] if partial is None else [partial]

    def body(place, *refs):
        ins, w_ref, out_ref = refs[:n_in], refs[n_in], refs[n_in + 1 + len(kept)]
        rows, w_vm, out_vm, row_sems, w_sems, out_sems = refs[-6:]
        put, fetch, send = [], [], []
        for i, (r, d) in enumerate(sides(n_u)):
            src, share = (ins[i], share_at(place, r, d, n_u)) if apart else (ins[0].at[i], i)
            cols = pl.ds(pl.multiple_of(share * DH, DH), DH)
            put.append(pltpu.make_async_copy(src, rows.at[:, cols], row_sems.at[i]))
        for t in range(n_tiles):
            for k in range(n_chunks):
                cols = pl.ds(t * tile, tile)
                src = w_ref.at[pl.ds(slot * depth + k * chunk, chunk), cols]
                dst = w_vm.at[pl.ds(k * chunk, chunk), cols]
                fetch.append(pltpu.make_async_copy(src, dst, w_sems.at[t, k]))
        for c in put + fetch:
            c.start()
        for c in put:
            c.wait()
        for t in range(n_tiles):
            cols = pl.ds(t * tile, tile)
            for c in fetch[t * n_chunks : (t + 1) * n_chunks]:
                c.wait()
            total = jnp.dot(rows[...], w_vm[:, cols], preferred_element_type=jnp.float32)
            if kept:
                total = total + refs[n_in + 1][:, cols]
            if last:
                out_vm[:, cols] = total.astype(jnp.bfloat16)
                send.append(
                    pltpu.make_async_copy(out_vm.at[:, cols], out_ref.at[:, cols], out_sems.at[t])
                )
                send[-1].start()
            else:
                out_ref[:, cols] = total
        for c in send:
            c.wait()

    return pl.pallas_call(
        body,
        out_shape=jax.ShapeDtypeStruct((T, width), jnp.bfloat16 if last else jnp.float32),
        in_specs=[SMEM] + [ANY] * (n_in + 1) + [VMEM] * len(kept),
        out_specs=ANY if last else VMEM,
        scratch_shapes=[
            pltpu.VMEM((T, depth), jnp.bfloat16),
            pltpu.VMEM((depth, width), weight.dtype),
            pltpu.VMEM((T, width if last else DH), jnp.bfloat16),
            pltpu.SemaphoreType.DMA((shares,)),
            pltpu.SemaphoreType.DMA((n_tiles, n_chunks)),
            pltpu.SemaphoreType.DMA((n_tiles,)),
        ],
        compiler_params=beside(4 * T * width + 10 * MIB),
        cost_estimate=cost(7),
        name="project",
    )(place, *arrays, weight, *kept)


def key_table(rand_blocks, chip, n_u, n_p, per):
    total = rand_blocks.shape[0]
    z = jnp.arange(n_u, dtype=jnp.int32)[:, None, None]
    core = jnp.arange(2, dtype=jnp.int32)[None, :, None]
    j = jnp.arange(per, dtype=jnp.int32)[None, None, :]
    mine = (((2 * chip + core) * n_u + z) * per + j).reshape(-1)
    window = jnp.stack([(mine - 1) % total, mine, (mine + 1) % total], axis=1)
    leading = jnp.broadcast_to(jnp.arange(GLOB, dtype=jnp.int32)[None, :], (mine.shape[0], GLOB))
    listed = jnp.concatenate([window, leading, rand_blocks[mine]], axis=1)
    device, inner = listed // per, listed % per
    zs, cs = device % n_u, device // n_u
    return ((((cs // 2) ^ chip) * n_u + zs) * 2 + cs % 2) * per + inner


def shards(queries, keys, values, rand_blocks, out_weight):
    n_c, n_u = lax.axis_size("ctx"), lax.axis_size("ulys")
    T, lanes = queries.shape
    hp = lanes // DH // (2 * n_u)
    c, z = lax.axis_index("ctx"), lax.axis_index("ulys")
    chip, core = c // 2, c % 2
    place = jnp.stack([z, core]).astype(jnp.int32)
    table = key_table(rand_blocks, chip, n_u, n_c // 2, T // BLK)

    q_of, kv, after = [], [], (table,)
    here = send_all(pack_sides(place, [keys, values], [0, 0], n_u), n_c, n_u, 1)
    for h in range(hp):
        if h < hp - 1:
            tensors, slots = [keys, values, queries], [h + 1, h + 1, h]
        else:
            tensors, slots = [queries], [h]
        first, second, packed = stage(place, here, tensors, slots, n_u, after)
        here = to_shares(packed, n_c, n_u)
        q_of.append((here, len(tensors) - 1))
        kv.append(gather_chips(first, second, n_c))
        after = [x for side in kv[-1] for x in side[1:]]

    total = None
    for h in range(hp):
        last = h == hp - 1
        parts = attend(place, table, *q_of[h], *kv[h], n_u, last)
        parts = send_all(parts, n_c, n_u, -1) if last else to_shares(parts[0], n_c, n_u)
        total = project(place, parts, out_weight, h, n_u, hp, total)
    return total


def solution(mesh):
    return jax.shard_map(
        shards,
        mesh=mesh,
        in_specs=(
            P(("ctx", "ulys"), None),
            P(("ctx", "ulys"), None),
            P(("ctx", "ulys"), None),
            P(),
            P(),
        ),
        out_specs=P(("ctx", "ulys"), None),
        check_vma=False,
    )
```

```python
import functools

import jax
import jax.numpy as jnp
from jax import lax
from jax.experimental import pallas as pl
from jax.experimental.pallas import tpu as pltpu
from jax.sharding import PartitionSpec as P

DH = 128
BLK = 64
GLOB = 2
RAND = 3
MIB = 1 << 20
LOG2E = 1.4426950408889634

ANY = pl.BlockSpec(memory_space=pl.ANY)
VMEM = pl.BlockSpec(memory_space=pltpu.VMEM)


WHOLE = pltpu.CompilerParams(vmem_limit_bytes=60 * MIB)


def beside(n_bytes):
    return pltpu.CompilerParams(vmem_limit_bytes=60 * MIB - n_bytes)


def cost(us):
    return pl.CostEstimate(flops=us * 1_150_000_000, bytes_accessed=0, transcendentals=0)


def copy_all(pairs, sems):
    copies = [pltpu.make_async_copy(src, dst, sems.at[i]) for i, (src, dst) in enumerate(pairs)]
    for c in copies:
        c.start()
    for c in copies:
        c.wait()


def sides(n_u):
    return [(r, d) for d in range(n_u) for r in range(2)]


def share_at(r, d, n_u):
    z, core = lax.axis_index("ulys"), lax.rem(lax.axis_index("ctx"), 2)
    return 2 * lax.rem(z + d + n_u, n_u) + (core if r == 0 else 1 - core)


def pack_first(tensors, n_u, early):
    T, nb, n_s = tensors[0].shape[0], len(tensors), 2 * n_u
    counts = [nb * (2 if early and d == 0 else 1) for _, d in sides(n_u)]

    def body(*refs):
        ins, outs = refs[:nb], refs[nb : nb + n_s]
        held, near, in_sems, out_sems = refs[nb + n_s :]
        pairs = [(ins[i].at[:, pl.ds(0, n_s * DH)], held.at[i]) for i in range(nb)]
        if early:
            cols = pl.ds(pl.multiple_of((n_s + 2 * lax.axis_index("ulys")) * DH, DH), 2 * DH)
            pairs += [(ins[i].at[:, cols], near.at[i]) for i in range(nb)]
        copy_all(pairs, in_sems)
        pairs = []
        for out, (r, d), count in zip(outs, sides(n_u), counts):
            at = pl.multiple_of(share_at(r, d, n_u) * DH, DH)
            pairs += [(held.at[i, :, pl.ds(at, DH)], out.at[i]) for i in range(nb)]
            if count > nb:
                at = pl.multiple_of((lax.rem(lax.axis_index("ctx"), 2) if r == 0 else 1 - lax.rem(lax.axis_index("ctx"), 2)) * DH, DH)
                pairs += [(near.at[i, :, pl.ds(at, DH)], out.at[nb + i]) for i in range(nb)]
        copy_all(pairs, out_sems)

    return pl.pallas_call(
        body,
        out_shape=[jax.ShapeDtypeStruct((n, T, DH), jnp.bfloat16) for n in counts],
        in_specs=[ANY] * nb,
        out_specs=[ANY] * n_s,
        scratch_shapes=[
            pltpu.VMEM((nb, T, n_s * DH), jnp.bfloat16),
            pltpu.VMEM((nb, T, 2 * DH), jnp.bfloat16),
            pltpu.SemaphoreType.DMA((2 * nb,)),
            pltpu.SemaphoreType.DMA((sum(counts),)),
        ],
        compiler_params=WHOLE,
        cost_estimate=cost(3),
        name="pack_first",
    )(*tensors)


def pack_rest(tensors, bundles, n_u, after):
    T, nb, n_s = tensors[0].shape[0], len(tensors), 2 * n_u
    items = [item for bundle in bundles for item in bundle]

    def body(*refs):
        ins, outs = refs[:nb], refs[nb + 1 : nb + 1 + len(bundles)]
        held, in_sems, out_sems = refs[nb + 1 + len(bundles) :]
        pairs, where = [], [(b, i) for b, bundle in enumerate(bundles) for i in range(len(bundle))]
        for n, (which, slot) in enumerate(items):
            pairs.append((ins[which].at[:, pl.ds(slot * n_s * DH, n_s * DH)], held.at[n]))
        copy_all(pairs, in_sems)
        pairs = []
        for n, (b, i) in enumerate(where):
            for k in range(n_s):
                pairs.append((held.at[n, :, pl.ds(k * DH, DH)], outs[b].at[k, i]))
        copy_all(pairs, out_sems)

    return pl.pallas_call(
        body,
        out_shape=[jax.ShapeDtypeStruct((n_s, len(b), T, DH), jnp.bfloat16) for b in bundles],
        in_specs=[ANY] * (nb + 1),
        out_specs=[ANY] * len(bundles),
        scratch_shapes=[
            pltpu.VMEM((len(items), T, n_s * DH), jnp.bfloat16),
            pltpu.SemaphoreType.DMA((len(items),)),
            pltpu.SemaphoreType.DMA((len(items) * n_s,)),
        ],
        compiler_params=WHOLE,
        cost_estimate=cost(3),
        name="pack_rest",
    )(*tensors, after)


def stage(here, packed, n_u, rest, after):
    apart = isinstance(here, list)
    blocks = here if apart else [here]
    n_s, n_b, T = 2 * n_u, len(blocks), blocks[0].shape[-2]
    n_early = blocks[0].shape[0] - 2 if apart else 0
    shapes = [((n_s - 2 * rest) * T, DH)] * 2 + [(2 * T, DH)] * n_early
    n_copies = sum(x.shape[0] for x in blocks) if apart else 2 * (n_s - 2 * rest)
    n_in, n_out = n_b + 1 + len(after), len(shapes)

    def body(*refs):
        z, core = lax.axis_index("ulys"), lax.rem(lax.axis_index("ctx"), 2)
        outs, sems = refs[n_in : n_in + n_out], refs[-1]
        pairs = []
        if apart:
            for k, (r, d) in enumerate(sides(n_u)):
                at = (2 * ((n_u - d) % n_u) + (core if r == 0 else 1 - core)) * T
                for i in range(blocks[k].shape[0]):
                    pairs.append((refs[k].at[i], outs[i].at[pl.ds(pl.multiple_of(at, T), T)]))
        else:
            for d in range(rest, n_u):
                for c in range(2):
                    src, at = 2 * lax.rem(z + d, n_u) + c, (2 * (d - rest) + c) * T
                    for i in range(2):
                        pairs.append((refs[0].at[src, i], outs[i].at[pl.ds(at, T)]))
        copy_all(pairs, sems)

    return pl.pallas_call(
        body,
        out_shape=[jax.ShapeDtypeStruct(x, jnp.bfloat16) for x in [*shapes, packed.shape]],
        in_specs=[ANY] * n_in,
        out_specs=[VMEM] * n_out + [ANY],
        input_output_aliases={n_b: n_out},
        scratch_shapes=[pltpu.SemaphoreType.DMA((n_copies,))],
        compiler_params=WHOLE,
        cost_estimate=cost(3),
        name="stage",
    )(*blocks, packed, *after)


def to_shares(x, n_c, n_u):
    groups = [
        [(2 * p + core) * n_u + z for z in range(n_u) for core in range(2)] for p in range(n_c // 2)
    ]
    return lax.all_to_all(
        x, ("ctx", "ulys"), split_axis=0, concat_axis=0, tiled=True, axis_index_groups=groups
    )


def send(x, r, d, n_c, n_u):
    if (r, d) == (0, 0):
        return x
    pairs = [(c * n_u + z, (c ^ r) * n_u + (z + d) % n_u) for c in range(n_c) for z in range(n_u)]
    return lax.ppermute(x, ("ctx", "ulys"), pairs)


def send_all(parts, n_c, n_u, sign):
    return [send(x, r, (sign * d) % n_u, n_c, n_u) for x, (r, d) in zip(parts, sides(n_u))]


def swap_chip(x, bit, n_c):
    return lax.ppermute(x, "ctx", [(i, i ^ (2 * bit)) for i in range(n_c)])


def gather_chips(first, second, n_c):
    n_p = n_c // 2
    bits = [1 << i for i in range(n_p.bit_length() - 1)]
    a, b = {0: first}, {0: second}
    for t in reversed(bits):
        a[t] = swap_chip(first, t, n_c)
    for t in bits:
        b[t] = swap_chip(second, t, n_c)
    for t in range(1, n_p):
        if t not in bits:
            low, high = t & -t, 1 << (t.bit_length() - 1)
            a[t] = swap_chip(a[t ^ low], low, n_c)
            b[t] = swap_chip(b[t ^ high], high, n_c)
    return [a[t] for t in range(n_p)], [b[t] for t in range(n_p)]


def attend(table, queries, q_index, keys, values, n_u, apart):
    n_s, _, T, _ = queries.shape
    n_q = n_s * T
    span = n_s * T
    n_k = span * len(keys)
    k_parts = [(x, t * span + at) for t, parts in enumerate(keys) for x, at in parts]
    v_parts = [(x, t * span + at) for t, parts in enumerate(values) for x, at in parts]
    n_rows, n_list = table.shape
    group = 4 * T // BLK
    arrays = [queries, *(x for x, _ in k_parts + v_parts)]
    n_in, n_out = len(arrays), 2 * n_u if apart else 1

    def body(table_ref, *refs):
        ins, outs = refs[:n_in], refs[n_in : n_in + n_out]
        table, q_vm, k_vm, v_vm, o_vm, sems, out_sems = refs[n_in + n_out :]
        pairs = [(table_ref, table)]
        for k in range(n_s):
            pairs.append((ins[0].at[k, q_index], q_vm.at[pl.ds(k * T, T)]))
        for i, (ref, (x, at)) in enumerate(zip(ins[1:], k_parts + v_parts)):
            vm = k_vm if i < len(k_parts) else v_vm
            pairs.append((ref, vm.at[pl.ds(at, x.shape[0])]))
        copies = [pltpu.make_async_copy(a, b, sems.at[i]) for i, (a, b) in enumerate(pairs)]
        for c in copies:
            c.start()
        for c in copies[: 1 + n_s + len(k_parts)]:
            c.wait()
        for step in range(n_rows // group):
            rows = range(step * group, (step + 1) * group)
            at = [[pl.multiple_of(table[r, j] * BLK, BLK) for j in range(n_list)] for r in rows]
            s = []
            for r, listed in zip(rows, at):
                k = jnp.concatenate([k_vm[pl.ds(a, BLK), :] for a in listed], axis=0)
                s.append(
                    lax.dot_general(
                        q_vm[pl.ds(r * BLK, BLK), :],
                        k,
                        (((1,), (1,)), ((), ())),
                        preferred_element_type=jnp.float32,
                    )
                )
            s = jnp.concatenate(s, axis=0)
            e = jnp.exp2((s - jnp.max(s, axis=-1, keepdims=True)) * (DH**-0.5 * LOG2E))
            w = (e * (1.0 / jnp.sum(e, axis=-1, keepdims=True))).astype(jnp.bfloat16)
            if step == 0:
                for c in copies[1 + n_s + len(k_parts) :]:
                    c.wait()
            for g, (r, listed) in enumerate(zip(rows, at)):
                v = jnp.concatenate([v_vm[pl.ds(a, BLK), :] for a in listed], axis=0)
                o = jnp.dot(
                    w[g * BLK : (g + 1) * BLK], v, preferred_element_type=jnp.float32
                )
                o_vm[pl.ds(r * BLK, BLK), :] = o.astype(jnp.bfloat16)

        pairs = []
        if apart:
            for out, (r, d) in zip(outs, sides(n_u)):
                at = pl.multiple_of(share_at(r, -d, n_u) * T, T)
                pairs.append((o_vm.at[pl.ds(at, T)], out))
        else:
            for k in range(n_s):
                pairs.append((o_vm.at[pl.ds(k * T, T)], outs[0].at[k]))
        copy_all(pairs, out_sems)

    return pl.pallas_call(
        body,
        out_shape=[jax.ShapeDtypeStruct((T, DH) if apart else (n_s, T, DH), jnp.bfloat16)] * n_out,
        in_specs=[ANY] * (1 + n_in),
        out_specs=[ANY] * n_out,
        scratch_shapes=[
            pltpu.SMEM(table.shape, jnp.int32),
            pltpu.VMEM((n_q, DH), jnp.bfloat16),
            pltpu.VMEM((n_k, DH), jnp.bfloat16),
            pltpu.VMEM((n_k, DH), jnp.bfloat16),
            pltpu.VMEM((n_q, DH), jnp.bfloat16),
            pltpu.SemaphoreType.DMA((n_s + n_in,)),
            pltpu.SemaphoreType.DMA((n_s,)),
        ],
        compiler_params=WHOLE,
        cost_estimate=cost(8),
        name="attend",
    )(table, *arrays)


def project(parts, weight, slot, n_u, hp, partial):
    apart, last = isinstance(parts, list), slot == hp - 1
    arrays = parts if apart else [parts]
    T = arrays[0].shape[-2]
    width = weight.shape[1]
    shares = 2 * n_u
    depth = shares * DH
    n_tiles, n_chunks = 2, 1
    tile, chunk = width // n_tiles, depth // n_chunks
    n_in = len(arrays)
    kept = [] if partial is None else [partial]

    def body(*refs):
        ins, w_ref, out_ref = refs[:n_in], refs[n_in], refs[n_in + 1 + len(kept)]
        rows, w_vm, out_vm, row_sems, w_sems, out_sems = refs[-6:]
        put, fetch, send = [], [], []
        for i, (r, d) in enumerate(sides(n_u)):
            src, share = (ins[i], share_at(r, d, n_u)) if apart else (ins[0].at[i], i)
            cols = pl.ds(pl.multiple_of(share * DH, DH), DH)
            put.append(pltpu.make_async_copy(src, rows.at[:, cols], row_sems.at[i]))
        for t in range(n_tiles):
            for k in range(n_chunks):
                cols = pl.ds(t * tile, tile)
                src = w_ref.at[pl.ds(slot * depth + k * chunk, chunk), cols]
                dst = w_vm.at[pl.ds(k * chunk, chunk), cols]
                fetch.append(pltpu.make_async_copy(src, dst, w_sems.at[t, k]))
        for c in put + fetch:
            c.start()
        for c in put:
            c.wait()
        for t in range(n_tiles):
            cols = pl.ds(t * tile, tile)
            for c in fetch[t * n_chunks : (t + 1) * n_chunks]:
                c.wait()
            total = jnp.dot(rows[...], w_vm[:, cols], preferred_element_type=jnp.float32)
            if kept:
                total = total + refs[n_in + 1][:, cols]
            if last:
                out_vm[:, cols] = total.astype(jnp.bfloat16)
                send.append(
                    pltpu.make_async_copy(out_vm.at[:, cols], out_ref.at[:, cols], out_sems.at[t])
                )
                send[-1].start()
            else:
                out_ref[:, cols] = total
        for c in send:
            c.wait()

    return pl.pallas_call(
        body,
        out_shape=jax.ShapeDtypeStruct((T, width), jnp.bfloat16 if last else jnp.float32),
        in_specs=[ANY] * (n_in + 1) + [VMEM] * len(kept),
        out_specs=ANY if last else VMEM,
        scratch_shapes=[
            pltpu.VMEM((T, depth), jnp.bfloat16),
            pltpu.VMEM((depth, width), weight.dtype),
            pltpu.VMEM((T, width if last else DH), jnp.bfloat16),
            pltpu.SemaphoreType.DMA((shares,)),
            pltpu.SemaphoreType.DMA((n_tiles, n_chunks)),
            pltpu.SemaphoreType.DMA((n_tiles,)),
        ],
        compiler_params=beside(4 * T * width + 10 * MIB),
        cost_estimate=cost(7),
        name="project",
    )(*arrays, weight, *kept)


def key_table(rand_blocks, chip, here, n_u, per):
    total = rand_blocks.shape[0]
    z = jnp.arange(n_u, dtype=jnp.int32)[:, None, None]
    core = jnp.arange(2, dtype=jnp.int32)[None, :, None]
    j = jnp.arange(per, dtype=jnp.int32)[None, None, :]
    mine = (((2 * chip + core) * n_u + z) * per + j).reshape(-1)
    window = jnp.stack([(mine - 1) % total, mine, (mine + 1) % total], axis=1)
    leading = jnp.broadcast_to(jnp.arange(GLOB, dtype=jnp.int32)[None, :], (mine.shape[0], GLOB))
    listed = jnp.concatenate([window, leading, rand_blocks[mine]], axis=1)
    device, inner = listed // per, listed % per
    zs, cs = device % n_u, device // n_u
    return ((((cs // 2) ^ chip) * n_u + (zs - here) % n_u) * 2 + cs % 2) * per + inner


def shards(queries, keys, values, rand_blocks, out_weight):
    n_c, n_u = lax.axis_size("ctx"), lax.axis_size("ulys")
    T, lanes = queries.shape
    hp = lanes // DH // (2 * n_u)
    c, z = lax.axis_index("ctx"), lax.axis_index("ulys")
    table = key_table(rand_blocks, c // 2, z, n_u, T // BLK)

    early = False
    bundles = [[(1, h + 1), (2, h + 1), (0, h)] for h in range(hp - 1)] + [[(0, hp - 1)]]
    parts = pack_first([keys, values], n_u, early)
    here = send_all(parts, n_c, n_u, 1)
    packed = pack_rest([queries, keys, values], bundles, n_u, here[2])
    q_of, kv, near, after = [], [], None, [table]
    for h in range(hp):
        rest = early and h == 1
        *blocks, ready = stage(here, packed[h], n_u, int(rest), after)
        here = to_shares(ready, n_c, n_u)
        q_of.append((here, len(bundles[h]) - 1))
        gathered = gather_chips(blocks[0], blocks[1], n_c)
        kv.append(
            [
                [[(near[i][t], 0), (x, 2 * T)] if rest else [(x, 0)] for t, x in enumerate(side)]
                for i, side in enumerate(gathered)
            ]
        )
        after = [x for side in gathered for x in side[1:]]
        if len(blocks) > 2:
            near = gather_chips(blocks[2], blocks[3], n_c)
            after += [x for side in near for x in side[1:]]

    total = None
    for h in range(hp):
        last = h == hp - 1
        parts = attend(table, *q_of[h], *kv[h], n_u, last)
        parts = send_all(parts, n_c, n_u, -1) if last else to_shares(parts[0], n_c, n_u)
        total = project(parts, out_weight, h, n_u, hp, total)
    return total


def solution(mesh):
    return jax.shard_map(
        shards,
        mesh=mesh,
        in_specs=(
            P(("ctx", "ulys"), None),
            P(("ctx", "ulys"), None),
            P(("ctx", "ulys"), None),
            P(),
            P(),
        ),
        out_specs=P(("ctx", "ulys"), None),
        check_vma=False,
    )
```

```python
import functools

import jax
import jax.numpy as jnp
from jax import lax
from jax.experimental import pallas as pl
from jax.experimental.pallas import tpu as pltpu
from jax.sharding import PartitionSpec as P

DH = 128
BLK = 64
GLOB = 2
RAND = 3
MIB = 1 << 20
LOG2E = 1.4426950408889634

ANY = pl.BlockSpec(memory_space=pl.ANY)
VMEM = pl.BlockSpec(memory_space=pltpu.VMEM)


WHOLE = pltpu.CompilerParams(vmem_limit_bytes=60 * MIB)


def beside(n_bytes):
    return pltpu.CompilerParams(vmem_limit_bytes=60 * MIB - n_bytes)


def cost(us):
    return pl.CostEstimate(flops=us * 1_150_000_000, bytes_accessed=0, transcendentals=0)


def copy_all(pairs, sems):
    copies = [pltpu.make_async_copy(src, dst, sems.at[i]) for i, (src, dst) in enumerate(pairs)]
    for c in copies:
        c.start()
    for c in copies:
        c.wait()


def sides(n_u):
    return [(r, d) for d in range(n_u) for r in range(2)]


def share_at(r, d, n_u):
    z, core = lax.axis_index("ulys"), lax.rem(lax.axis_index("ctx"), 2)
    return 2 * lax.rem(z + d + n_u, n_u) + (core if r == 0 else 1 - core)


def pack_first(tensors, n_u, early):
    T, nb, n_s = tensors[0].shape[0], len(tensors), 2 * n_u
    counts = [nb * (2 if early and d == 0 else 1) for _, d in sides(n_u)]

    def body(*refs):
        ins, outs = refs[:nb], refs[nb : nb + n_s]
        held, near, in_sems, out_sems = refs[nb + n_s :]
        pairs = [(ins[i].at[:, pl.ds(0, n_s * DH)], held.at[i]) for i in range(nb)]
        if early:
            cols = pl.ds(pl.multiple_of((n_s + 2 * lax.axis_index("ulys")) * DH, DH), 2 * DH)
            pairs += [(ins[i].at[:, cols], near.at[i]) for i in range(nb)]
        copy_all(pairs, in_sems)
        pairs = []
        for out, (r, d), count in zip(outs, sides(n_u), counts):
            at = pl.multiple_of(share_at(r, d, n_u) * DH, DH)
            pairs += [(held.at[i, :, pl.ds(at, DH)], out.at[i]) for i in range(nb)]
            if count > nb:
                at = pl.multiple_of((lax.rem(lax.axis_index("ctx"), 2) if r == 0 else 1 - lax.rem(lax.axis_index("ctx"), 2)) * DH, DH)
                pairs += [(near.at[i, :, pl.ds(at, DH)], out.at[nb + i]) for i in range(nb)]
        copy_all(pairs, out_sems)

    return pl.pallas_call(
        body,
        out_shape=[jax.ShapeDtypeStruct((n, T, DH), jnp.bfloat16) for n in counts],
        in_specs=[ANY] * nb,
        out_specs=[ANY] * n_s,
        scratch_shapes=[
            pltpu.VMEM((nb, T, n_s * DH), jnp.bfloat16),
            pltpu.VMEM((nb, T, 2 * DH), jnp.bfloat16),
            pltpu.SemaphoreType.DMA((2 * nb,)),
            pltpu.SemaphoreType.DMA((sum(counts),)),
        ],
        compiler_params=beside(8 * MIB),
        cost_estimate=cost(3),
        name="pack_first",
    )(*tensors)


def pack_rest(tensors, bundles, n_u, after):
    T, nb, n_s = tensors[0].shape[0], len(tensors), 2 * n_u
    items = [item for bundle in bundles for item in bundle]

    def body(*refs):
        ins, outs = refs[:nb], refs[nb + 1 : nb + 1 + len(bundles)]
        held, in_sems, out_sems = refs[nb + 1 + len(bundles) :]
        pairs, where = [], [(b, i) for b, bundle in enumerate(bundles) for i in range(len(bundle))]
        for n, (which, slot) in enumerate(items):
            pairs.append((ins[which].at[:, pl.ds(slot * n_s * DH, n_s * DH)], held.at[n]))
        copy_all(pairs, in_sems)
        pairs = []
        for n, (b, i) in enumerate(where):
            for k in range(n_s):
                pairs.append((held.at[n, :, pl.ds(k * DH, DH)], outs[b].at[k, i]))
        copy_all(pairs, out_sems)

    return pl.pallas_call(
        body,
        out_shape=[jax.ShapeDtypeStruct((n_s, len(b), T, DH), jnp.bfloat16) for b in bundles],
        in_specs=[ANY] * (nb + 1),
        out_specs=[ANY] * len(bundles),
        scratch_shapes=[
            pltpu.VMEM((len(items), T, n_s * DH), jnp.bfloat16),
            pltpu.SemaphoreType.DMA((len(items),)),
            pltpu.SemaphoreType.DMA((len(items) * n_s,)),
        ],
        compiler_params=beside(8 * MIB),
        cost_estimate=cost(3),
        name="pack_rest",
    )(*tensors, after)


def stage(here, packed, n_u, rest, after):
    apart = isinstance(here, list)
    blocks = here if apart else [here]
    n_s, n_b, T = 2 * n_u, len(blocks), blocks[0].shape[-2]
    n_early = blocks[0].shape[0] - 2 if apart else 0
    shapes = [((n_s - 2 * rest) * T, DH)] * 2 + [(2 * T, DH)] * n_early
    n_copies = sum(x.shape[0] for x in blocks) if apart else 2 * (n_s - 2 * rest)
    n_in, n_out = n_b + 1 + len(after), len(shapes)

    def body(*refs):
        z, core = lax.axis_index("ulys"), lax.rem(lax.axis_index("ctx"), 2)
        outs, sems = refs[n_in : n_in + n_out], refs[-1]
        pairs = []
        if apart:
            for k, (r, d) in enumerate(sides(n_u)):
                at = (2 * ((n_u - d) % n_u) + (core if r == 0 else 1 - core)) * T
                for i in range(blocks[k].shape[0]):
                    pairs.append((refs[k].at[i], outs[i].at[pl.ds(pl.multiple_of(at, T), T)]))
        else:
            for d in range(rest, n_u):
                for c in range(2):
                    src, at = 2 * lax.rem(z + d, n_u) + c, (2 * (d - rest) + c) * T
                    for i in range(2):
                        pairs.append((refs[0].at[src, i], outs[i].at[pl.ds(at, T)]))
        copy_all(pairs, sems)

    return pl.pallas_call(
        body,
        out_shape=[jax.ShapeDtypeStruct(x, jnp.bfloat16) for x in [*shapes, packed.shape]],
        in_specs=[ANY] * n_in,
        out_specs=[VMEM] * n_out + [ANY],
        input_output_aliases={n_b: n_out},
        scratch_shapes=[pltpu.SemaphoreType.DMA((n_copies,))],
        compiler_params=beside(8 * MIB),
        cost_estimate=cost(3),
        name="stage",
    )(*blocks, packed, *after)


def to_shares(x, n_c, n_u):
    groups = [
        [(2 * p + core) * n_u + z for z in range(n_u) for core in range(2)] for p in range(n_c // 2)
    ]
    return lax.all_to_all(
        x, ("ctx", "ulys"), split_axis=0, concat_axis=0, tiled=True, axis_index_groups=groups
    )


def send(x, r, d, n_c, n_u):
    if (r, d) == (0, 0):
        return x
    pairs = [(c * n_u + z, (c ^ r) * n_u + (z + d) % n_u) for c in range(n_c) for z in range(n_u)]
    return lax.ppermute(x, ("ctx", "ulys"), pairs)


def send_all(parts, n_c, n_u, sign):
    return [send(x, r, (sign * d) % n_u, n_c, n_u) for x, (r, d) in zip(parts, sides(n_u))]


def swap_chip(x, bit, n_c):
    return lax.ppermute(x, "ctx", [(i, i ^ (2 * bit)) for i in range(n_c)])


def gather_chips(first, second, n_c):
    n_p = n_c // 2
    bits = [1 << i for i in range(n_p.bit_length() - 1)]
    a, b = {0: first}, {0: second}
    for t in reversed(bits):
        a[t] = swap_chip(first, t, n_c)
    for t in bits:
        b[t] = swap_chip(second, t, n_c)
    for t in range(1, n_p):
        if t not in bits:
            low, high = t & -t, 1 << (t.bit_length() - 1)
            a[t] = swap_chip(a[t ^ low], low, n_c)
            b[t] = swap_chip(b[t ^ high], high, n_c)
    return [a[t] for t in range(n_p)], [b[t] for t in range(n_p)]


def attend(table, queries, q_index, keys, values, n_u, apart):
    n_s, _, T, _ = queries.shape
    n_q = n_s * T
    span = n_s * T
    n_k = span * len(keys)
    k_parts = [(x, t * span + at) for t, parts in enumerate(keys) for x, at in parts]
    v_parts = [(x, t * span + at) for t, parts in enumerate(values) for x, at in parts]
    n_rows, n_list = table.shape
    group = 4 * T // BLK
    arrays = [queries, *(x for x, _ in k_parts + v_parts)]
    n_in, n_out = len(arrays), 2 * n_u if apart else 1

    def body(table_ref, *refs):
        ins, outs = refs[:n_in], refs[n_in : n_in + n_out]
        table, q_vm, k_vm, v_vm, o_vm, sems, out_sems = refs[n_in + n_out :]
        pairs = [(table_ref, table)]
        for k in range(n_s):
            pairs.append((ins[0].at[k, q_index], q_vm.at[pl.ds(k * T, T)]))
        for i, (ref, (x, at)) in enumerate(zip(ins[1:], k_parts + v_parts)):
            vm = k_vm if i < len(k_parts) else v_vm
            pairs.append((ref, vm.at[pl.ds(at, x.shape[0])]))
        copies = [pltpu.make_async_copy(a, b, sems.at[i]) for i, (a, b) in enumerate(pairs)]
        for c in copies:
            c.start()
        for c in copies[: 1 + n_s + len(k_parts)]:
            c.wait()
        for step in range(n_rows // group):
            rows = range(step * group, (step + 1) * group)
            at = [[pl.multiple_of(table[r, j] * BLK, BLK) for j in range(n_list)] for r in rows]
            s = []
            for r, listed in zip(rows, at):
                k = jnp.concatenate([k_vm[pl.ds(a, BLK), :] for a in listed], axis=0)
                s.append(
                    lax.dot_general(
                        q_vm[pl.ds(r * BLK, BLK), :],
                        k,
                        (((1,), (1,)), ((), ())),
                        preferred_element_type=jnp.float32,
                    )
                )
            s = jnp.concatenate(s, axis=0)
            e = jnp.exp2((s - jnp.max(s, axis=-1, keepdims=True)) * (DH**-0.5 * LOG2E))
            w = (e * (1.0 / jnp.sum(e, axis=-1, keepdims=True))).astype(jnp.bfloat16)
            if step == 0:
                for c in copies[1 + n_s + len(k_parts) :]:
                    c.wait()
            for g, (r, listed) in enumerate(zip(rows, at)):
                v = jnp.concatenate([v_vm[pl.ds(a, BLK), :] for a in listed], axis=0)
                o = jnp.dot(
                    w[g * BLK : (g + 1) * BLK], v, preferred_element_type=jnp.float32
                )
                o_vm[pl.ds(r * BLK, BLK), :] = o.astype(jnp.bfloat16)

        pairs = []
        if apart:
            for out, (r, d) in zip(outs, sides(n_u)):
                at = pl.multiple_of(share_at(r, -d, n_u) * T, T)
                pairs.append((o_vm.at[pl.ds(at, T)], out))
        else:
            for k in range(n_s):
                pairs.append((o_vm.at[pl.ds(k * T, T)], outs[0].at[k]))
        copy_all(pairs, out_sems)

    return pl.pallas_call(
        body,
        out_shape=[jax.ShapeDtypeStruct((T, DH) if apart else (n_s, T, DH), jnp.bfloat16)] * n_out,
        in_specs=[ANY] * (1 + n_in),
        out_specs=[ANY] * n_out,
        scratch_shapes=[
            pltpu.SMEM(table.shape, jnp.int32),
            pltpu.VMEM((n_q, DH), jnp.bfloat16),
            pltpu.VMEM((n_k, DH), jnp.bfloat16),
            pltpu.VMEM((n_k, DH), jnp.bfloat16),
            pltpu.VMEM((n_q, DH), jnp.bfloat16),
            pltpu.SemaphoreType.DMA((n_s + n_in,)),
            pltpu.SemaphoreType.DMA((n_s,)),
        ],
        compiler_params=WHOLE,
        cost_estimate=cost(8),
        name="attend",
    )(table, *arrays)


def project(parts, weight, slot, n_u, hp, partial):
    apart, last = isinstance(parts, list), slot == hp - 1
    arrays = parts if apart else [parts]
    T = arrays[0].shape[-2]
    width = weight.shape[1]
    shares = 2 * n_u
    depth = shares * DH
    n_tiles, n_chunks = 2, 1
    tile, chunk = width // n_tiles, depth // n_chunks
    n_in = len(arrays)
    kept = [] if partial is None else [partial]

    def body(*refs):
        ins, w_ref, out_ref = refs[:n_in], refs[n_in], refs[n_in + 1 + len(kept)]
        rows, w_vm, out_vm, row_sems, w_sems, out_sems = refs[-6:]
        put, fetch, send = [], [], []
        for i, (r, d) in enumerate(sides(n_u)):
            src, share = (ins[i], share_at(r, d, n_u)) if apart else (ins[0].at[i], i)
            cols = pl.ds(pl.multiple_of(share * DH, DH), DH)
            put.append(pltpu.make_async_copy(src, rows.at[:, cols], row_sems.at[i]))
        for t in range(n_tiles):
            for k in range(n_chunks):
                cols = pl.ds(t * tile, tile)
                src = w_ref.at[pl.ds(slot * depth + k * chunk, chunk), cols]
                dst = w_vm.at[pl.ds(k * chunk, chunk), cols]
                fetch.append(pltpu.make_async_copy(src, dst, w_sems.at[t, k]))
        for c in put + fetch:
            c.start()
        for c in put:
            c.wait()
        for t in range(n_tiles):
            cols = pl.ds(t * tile, tile)
            for c in fetch[t * n_chunks : (t + 1) * n_chunks]:
                c.wait()
            total = jnp.dot(rows[...], w_vm[:, cols], preferred_element_type=jnp.float32)
            if kept:
                total = total + refs[n_in + 1][:, cols]
            if last:
                out_vm[:, cols] = total.astype(jnp.bfloat16)
                send.append(
                    pltpu.make_async_copy(out_vm.at[:, cols], out_ref.at[:, cols], out_sems.at[t])
                )
                send[-1].start()
            else:
                out_ref[:, cols] = total
        for c in send:
            c.wait()

    return pl.pallas_call(
        body,
        out_shape=jax.ShapeDtypeStruct((T, width), jnp.bfloat16 if last else jnp.float32),
        in_specs=[ANY] * (n_in + 1) + [VMEM] * len(kept),
        out_specs=ANY if last else VMEM,
        scratch_shapes=[
            pltpu.VMEM((T, depth), jnp.bfloat16),
            pltpu.VMEM((depth, width), weight.dtype),
            pltpu.VMEM((T, width if last else DH), jnp.bfloat16),
            pltpu.SemaphoreType.DMA((shares,)),
            pltpu.SemaphoreType.DMA((n_tiles, n_chunks)),
            pltpu.SemaphoreType.DMA((n_tiles,)),
        ],
        compiler_params=beside(4 * T * width + 10 * MIB),
        cost_estimate=cost(7),
        name="project",
    )(*arrays, weight, *kept)


def key_table(rand_blocks, chip, here, n_u, per):
    total = rand_blocks.shape[0]
    z = jnp.arange(n_u, dtype=jnp.int32)[:, None, None]
    core = jnp.arange(2, dtype=jnp.int32)[None, :, None]
    j = jnp.arange(per, dtype=jnp.int32)[None, None, :]
    mine = (((2 * chip + core) * n_u + z) * per + j).reshape(-1)
    window = jnp.stack([(mine - 1) % total, mine, (mine + 1) % total], axis=1)
    leading = jnp.broadcast_to(jnp.arange(GLOB, dtype=jnp.int32)[None, :], (mine.shape[0], GLOB))
    listed = jnp.concatenate([window, leading, rand_blocks[mine]], axis=1)
    device, inner = listed // per, listed % per
    zs, cs = device % n_u, device // n_u
    return ((((cs // 2) ^ chip) * n_u + (zs - here) % n_u) * 2 + cs % 2) * per + inner


def shards(queries, keys, values, rand_blocks, out_weight):
    n_c, n_u = lax.axis_size("ctx"), lax.axis_size("ulys")
    T, lanes = queries.shape
    hp = lanes // DH // (2 * n_u)
    c, z = lax.axis_index("ctx"), lax.axis_index("ulys")
    table = key_table(rand_blocks, c // 2, z, n_u, T // BLK)

    early = False
    bundles = [[(1, h + 1), (2, h + 1), (0, h)] for h in range(hp - 1)] + [[(0, hp - 1)]]
    parts = pack_first([keys, values], n_u, early)
    here = send_all(parts, n_c, n_u, 1)
    packed = pack_rest([queries, keys, values], bundles, n_u, here[2])
    q_of, kv, near, after = [], [], None, [table]
    for h in range(hp):
        rest = early and h == 1
        *blocks, ready = stage(here, packed[h], n_u, int(rest), after)
        here = to_shares(ready, n_c, n_u)
        q_of.append((here, len(bundles[h]) - 1))
        gathered = gather_chips(blocks[0], blocks[1], n_c)
        kv.append(
            [
                [[(near[i][t], 0), (x, 2 * T)] if rest else [(x, 0)] for t, x in enumerate(side)]
                for i, side in enumerate(gathered)
            ]
        )
        after = [x for side in gathered for x in side[1:]]
        if len(blocks) > 2:
            near = gather_chips(blocks[2], blocks[3], n_c)
            after += [x for side in near for x in side[1:]]

    total = None
    for h in range(hp):
        last = h == hp - 1
        parts = attend(table, *q_of[h], *kv[h], n_u, last)
        parts = send_all(parts, n_c, n_u, -1) if last else to_shares(parts[0], n_c, n_u)
        total = project(parts, out_weight, h, n_u, hp, total)
    return total


def solution(mesh):
    return jax.shard_map(
        shards,
        mesh=mesh,
        in_specs=(
            P(("ctx", "ulys"), None),
            P(("ctx", "ulys"), None),
            P(("ctx", "ulys"), None),
            P(),
            P(),
        ),
        out_specs=P(("ctx", "ulys"), None),
        check_vma=False,
    )
```

```python
import functools

import jax
import jax.numpy as jnp
from jax import lax
from jax.experimental import pallas as pl
from jax.experimental.pallas import tpu as pltpu
from jax.sharding import PartitionSpec as P

DH = 128
BLK = 64
GLOB = 2
RAND = 3
MIB = 1 << 20
LOG2E = 1.4426950408889634

ANY = pl.BlockSpec(memory_space=pl.ANY)
VMEM = pl.BlockSpec(memory_space=pltpu.VMEM)


WHOLE = pltpu.CompilerParams(vmem_limit_bytes=60 * MIB)


def beside(n_bytes):
    return pltpu.CompilerParams(vmem_limit_bytes=60 * MIB - n_bytes)


def cost(us):
    return pl.CostEstimate(flops=us * 1_150_000_000, bytes_accessed=0, transcendentals=0)


def copy_all(pairs, sems):
    copies = [pltpu.make_async_copy(src, dst, sems.at[i]) for i, (src, dst) in enumerate(pairs)]
    for c in copies:
        c.start()
    for c in copies:
        c.wait()


def sides(n_u):
    return [(r, d) for d in range(n_u) for r in range(2)]


def share_at(r, d, n_u):
    z, core = lax.axis_index("ulys"), lax.rem(lax.axis_index("ctx"), 2)
    return 2 * lax.rem(z + d + n_u, n_u) + (core if r == 0 else 1 - core)


def pack_first(tensors, n_u, hp):
    T, nb, n_s = tensors[0].shape[0], len(tensors), 2 * n_u

    def body(*refs):
        ins, outs = refs[:nb], refs[nb : nb + n_u + 1]
        held, near, in_sems, out_sems = refs[nb + n_u + 1 :]
        z, core = lax.axis_index("ulys"), lax.rem(lax.axis_index("ctx"), 2)
        pairs = [(ins[i].at[:, pl.ds(0, n_s * DH)], held.at[i]) for i in range(nb)]
        for h in range(hp):
            cols = pl.ds(pl.multiple_of((h * n_s + 2 * z) * DH, DH), 2 * DH)
            pairs += [(ins[i].at[:, cols], near.at[h * nb + i]) for i in range(nb)]
        copy_all(pairs, in_sems)
        pairs = []
        for r in range(2):
            for d in range(1, n_u):
                cols = pl.ds(pl.multiple_of(share_at(r, d, n_u) * DH, DH), DH)
                pairs += [(held.at[i, :, cols], outs[d - 1].at[r, i]) for i in range(nb)]
            cols = pl.ds(pl.multiple_of((core if r == 0 else 1 - core) * DH, DH), DH)
            pairs += [(near.at[i, :, cols], outs[n_u - 1 + r].at[i]) for i in range(hp * nb)]
        copy_all(pairs, out_sems)

    shapes = [(2, nb, T, DH)] * (n_u - 1) + [(hp * nb, T, DH)] * 2
    return pl.pallas_call(
        body,
        out_shape=[jax.ShapeDtypeStruct(x, jnp.bfloat16) for x in shapes],
        in_specs=[ANY] * nb,
        out_specs=[ANY] * (n_u + 1),
        scratch_shapes=[
            pltpu.VMEM((nb, T, n_s * DH), jnp.bfloat16),
            pltpu.VMEM((hp * nb, T, 2 * DH), jnp.bfloat16),
            pltpu.SemaphoreType.DMA(((1 + hp) * nb,)),
            pltpu.SemaphoreType.DMA(((n_s - 2 + 2 * hp) * nb,)),
        ],
        compiler_params=beside(8 * MIB),
        cost_estimate=cost(2),
        name="pack_first",
    )(*tensors)


def for_other(parts):
    n = len(parts)

    def body(*refs):
        copy_all([(refs[i].at[1], refs[n].at[i]) for i in range(n)], refs[n + 1])

    return pl.pallas_call(
        body,
        out_shape=jax.ShapeDtypeStruct((n, *parts[0].shape[1:]), jnp.bfloat16),
        in_specs=[ANY] * n,
        out_specs=VMEM,
        scratch_shapes=[pltpu.SemaphoreType.DMA((n,))],
        compiler_params=beside(8 * MIB),
        cost_estimate=cost(1),
        name="for_other",
    )(*parts)


def release(packed, after):
    def body(*refs):
        pass

    return pl.pallas_call(
        body,
        out_shape=jax.ShapeDtypeStruct(packed.shape, packed.dtype),
        in_specs=[ANY] * (1 + len(after)),
        out_specs=ANY,
        input_output_aliases={0: 0},
        compiler_params=WHOLE,
        cost_estimate=cost(1),
        name="release",
    )(packed, *after)


def join(mine, other, hp):
    n, T, _ = mine.shape
    nb = n // hp

    def body(mine_ref, other_ref, out, sems):
        core = lax.rem(lax.axis_index("ctx"), 2)
        pairs = []
        for r, ref in enumerate((mine_ref, other_ref)):
            for h in range(hp):
                for i in range(nb):
                    at = (2 * (i * hp + h) + (core if r == 0 else 1 - core)) * T
                    pairs.append((ref.at[h * nb + i], out.at[pl.ds(pl.multiple_of(at, T), T)]))
        copy_all(pairs, sems)

    return pl.pallas_call(
        body,
        out_shape=jax.ShapeDtypeStruct((2 * n * T, DH), jnp.bfloat16),
        in_specs=[ANY] * 2,
        out_specs=VMEM,
        scratch_shapes=[pltpu.SemaphoreType.DMA((2 * hp * nb,))],
        compiler_params=beside(8 * MIB),
        cost_estimate=cost(2),
        name="join",
    )(mine, other)


def pack_rest(tensors, bundles, n_u, after):
    T, nb, n_s = tensors[0].shape[0], len(tensors), 2 * n_u
    items = [item for bundle in bundles for item in bundle]

    def body(*refs):
        ins, outs = refs[:nb], refs[nb + 1 : nb + 1 + len(bundles)]
        held, in_sems, out_sems = refs[nb + 1 + len(bundles) :]
        pairs, where = [], [(b, i) for b, bundle in enumerate(bundles) for i in range(len(bundle))]
        for n, (which, slot) in enumerate(items):
            pairs.append((ins[which].at[:, pl.ds(slot * n_s * DH, n_s * DH)], held.at[n]))
        copy_all(pairs, in_sems)
        pairs = []
        for n, (b, i) in enumerate(where):
            for k in range(n_s):
                pairs.append((held.at[n, :, pl.ds(k * DH, DH)], outs[b].at[k, i]))
        copy_all(pairs, out_sems)

    return pl.pallas_call(
        body,
        out_shape=[jax.ShapeDtypeStruct((n_s, len(b), T, DH), jnp.bfloat16) for b in bundles],
        in_specs=[ANY] * (nb + 1),
        out_specs=[ANY] * len(bundles),
        scratch_shapes=[
            pltpu.VMEM((len(items), T, n_s * DH), jnp.bfloat16),
            pltpu.SemaphoreType.DMA((len(items),)),
            pltpu.SemaphoreType.DMA((len(items) * n_s,)),
        ],
        compiler_params=beside(8 * MIB),
        cost_estimate=cost(3),
        name="pack_rest",
    )(*tensors, after)


def stage(blocks, packed, n_u, after):
    n_s, n_b, T = 2 * n_u, len(blocks), blocks[0].shape[2]
    last = [] if packed is None else [packed]
    n_in = n_b + len(last) + len(after)

    def body(*refs):
        z, core = lax.axis_index("ulys"), lax.rem(lax.axis_index("ctx"), 2)
        outs, sems = refs[n_in : n_in + 2], refs[-1]
        pairs = []
        for k in range(2, n_s):
            d, c = k // 2, k % 2
            if n_b == 1:
                block, at = refs[0].at[2 * lax.rem(z + d, n_u) + c], (k - 2) * T
            else:
                block = refs[n_u - d - 1].at[0] if c == 0 else refs[n_b - 1].at[n_u - d - 1]
                at = (2 * (d - 1) + (core if c == 0 else 1 - core)) * T
            pairs += [(block.at[i], outs[i].at[pl.ds(pl.multiple_of(at, T), T)]) for i in range(2)]
        copy_all(pairs, sems)

    shapes = [((n_s - 2) * T, DH)] * 2 + [x.shape for x in last]
    return pl.pallas_call(
        body,
        out_shape=[jax.ShapeDtypeStruct(x, jnp.bfloat16) for x in shapes],
        in_specs=[ANY] * n_in,
        out_specs=[VMEM] * 2 + [ANY] * len(last),
        input_output_aliases={n_b: 2} if last else {},
        scratch_shapes=[pltpu.SemaphoreType.DMA((2 * (n_s - 2),))],
        compiler_params=beside(8 * MIB),
        cost_estimate=cost(3),
        name="stage",
    )(*blocks, *last, *after)


def to_shares(x, n_c, n_u):
    groups = [
        [(2 * p + core) * n_u + z for z in range(n_u) for core in range(2)] for p in range(n_c // 2)
    ]
    return lax.all_to_all(
        x, ("ctx", "ulys"), split_axis=0, concat_axis=0, tiled=True, axis_index_groups=groups
    )


def send(x, r, d, n_c, n_u):
    if (r, d) == (0, 0):
        return x
    pairs = [(c * n_u + z, (c ^ r) * n_u + (z + d) % n_u) for c in range(n_c) for z in range(n_u)]
    return lax.ppermute(x, ("ctx", "ulys"), pairs)


def send_all(parts, n_c, n_u, sign):
    return [send(x, r, (sign * d) % n_u, n_c, n_u) for x, (r, d) in zip(parts, sides(n_u))]


def swap_core(x, n_c):
    return lax.ppermute(x, "ctx", [(i, i ^ 1) for i in range(n_c)])


def swap_chip(x, bit, n_c):
    return lax.ppermute(x, "ctx", [(i, i ^ (2 * bit)) for i in range(n_c)])


def gather_whole(x, n_c):
    n_p, half = n_c // 2, x.shape[0] // 2
    got, halves = [], {0: [(x, 0), (x, half)]}

    def again(part, bit):
        y, at = part
        got.append(swap_chip(y if y.shape[0] == half else y[at : at + half], bit, n_c))
        return (got[-1], 0)

    for t in range(1, n_p):
        if t & (t - 1) == 0:
            got.append(swap_chip(x, t, n_c))
            halves[t] = [(got[-1], 0), (got[-1], half)]
    for t in range(1, n_p):
        if t & (t - 1) != 0:
            low, high = t & -t, 1 << (t.bit_length() - 1)
            halves[t] = [again(halves[t ^ low][0], low), again(halves[t ^ high][1], high)]
    return [[halves[t][i] for t in range(n_p)] for i in range(2)], got


def gather_chips(first, second, n_c):
    n_p = n_c // 2
    bits = [1 << i for i in range(n_p.bit_length() - 1)]
    a, b = {0: first}, {0: second}
    for t in reversed(bits):
        a[t] = swap_chip(first, t, n_c)
    for t in bits:
        b[t] = swap_chip(second, t, n_c)
    for t in range(1, n_p):
        if t not in bits:
            low, high = t & -t, 1 << (t.bit_length() - 1)
            a[t] = swap_chip(a[t ^ low], low, n_c)
            b[t] = swap_chip(b[t ^ high], high, n_c)
    return [a[t] for t in range(n_p)], [b[t] for t in range(n_p)]


def attend(table, queries, q_index, slot, near, far, n_u, apart):
    n_s, _, T, _ = queries.shape
    n_q = n_s * T
    span = n_s * T
    n_k = span * len(far[0])
    parts = []
    for nears, fars in zip(near, far):
        for t, ((x, at), y) in enumerate(zip(nears, fars)):
            parts.append((x, at + slot * 2 * T, t * span, 2 * T))
            parts.append((y, 0, t * span + 2 * T, span - 2 * T))
    n_half = len(parts) // 2
    n_rows, n_list = table.shape
    group = 4 * T // BLK
    arrays = [queries, *(x for x, _, _, _ in parts)]
    n_in, n_out = len(arrays), 2 * n_u if apart else 1

    def body(table_ref, *refs):
        ins, outs = refs[:n_in], refs[n_in : n_in + n_out]
        table, q_vm, k_vm, v_vm, o_vm, sems, out_sems = refs[n_in + n_out :]
        pairs = [(table_ref, table)]
        for k in range(n_s):
            pairs.append((ins[0].at[k, q_index], q_vm.at[pl.ds(k * T, T)]))
        for i, (ref, (_, src, dst, n)) in enumerate(zip(ins[1:], parts)):
            vm = k_vm if i < n_half else v_vm
            pairs.append((ref.at[pl.ds(src, n)], vm.at[pl.ds(dst, n)]))
        copies = [pltpu.make_async_copy(a, b, sems.at[i]) for i, (a, b) in enumerate(pairs)]
        for c in copies:
            c.start()
        for c in copies[: 1 + n_s + n_half]:
            c.wait()
        for step in range(n_rows // group):
            rows = range(step * group, (step + 1) * group)
            at = [[pl.multiple_of(table[r, j] * BLK, BLK) for j in range(n_list)] for r in rows]
            s = []
            for r, listed in zip(rows, at):
                k = jnp.concatenate([k_vm[pl.ds(a, BLK), :] for a in listed], axis=0)
                s.append(
                    lax.dot_general(
                        q_vm[pl.ds(r * BLK, BLK), :],
                        k,
                        (((1,), (1,)), ((), ())),
                        preferred_element_type=jnp.float32,
                    )
                )
            s = jnp.concatenate(s, axis=0)
            e = jnp.exp2((s - jnp.max(s, axis=-1, keepdims=True)) * (DH**-0.5 * LOG2E))
            w = (e * (1.0 / jnp.sum(e, axis=-1, keepdims=True))).astype(jnp.bfloat16)
            if step == 0:
                for c in copies[1 + n_s + n_half :]:
                    c.wait()
            for g, (r, listed) in enumerate(zip(rows, at)):
                v = jnp.concatenate([v_vm[pl.ds(a, BLK), :] for a in listed], axis=0)
                o = jnp.dot(
                    w[g * BLK : (g + 1) * BLK], v, preferred_element_type=jnp.float32
                )
                o_vm[pl.ds(r * BLK, BLK), :] = o.astype(jnp.bfloat16)

        pairs = []
        if apart:
            for out, (r, d) in zip(outs, sides(n_u)):
                at = pl.multiple_of(share_at(r, -d, n_u) * T, T)
                pairs.append((o_vm.at[pl.ds(at, T)], out))
        else:
            for k in range(n_s):
                pairs.append((o_vm.at[pl.ds(k * T, T)], outs[0].at[k]))
        copy_all(pairs, out_sems)

    return pl.pallas_call(
        body,
        out_shape=[jax.ShapeDtypeStruct((T, DH) if apart else (n_s, T, DH), jnp.bfloat16)] * n_out,
        in_specs=[ANY] * (1 + n_in),
        out_specs=[ANY] * n_out,
        scratch_shapes=[
            pltpu.SMEM(table.shape, jnp.int32),
            pltpu.VMEM((n_q, DH), jnp.bfloat16),
            pltpu.VMEM((n_k, DH), jnp.bfloat16),
            pltpu.VMEM((n_k, DH), jnp.bfloat16),
            pltpu.VMEM((n_q, DH), jnp.bfloat16),
            pltpu.SemaphoreType.DMA((n_s + n_in,)),
            pltpu.SemaphoreType.DMA((n_s,)),
        ],
        compiler_params=WHOLE,
        cost_estimate=cost(8),
        name="attend",
    )(table, *arrays)


def project(parts, weight, slot, n_u, hp, partial):
    apart, last = isinstance(parts, list), slot == hp - 1
    arrays = parts if apart else [parts]
    T = arrays[0].shape[-2]
    width = weight.shape[1]
    shares = 2 * n_u
    depth = shares * DH
    n_tiles, n_chunks = 2, 1
    tile, chunk = width // n_tiles, depth // n_chunks
    n_in = len(arrays)
    kept = [] if partial is None else [partial]

    def body(*refs):
        ins, w_ref, out_ref = refs[:n_in], refs[n_in], refs[n_in + 1 + len(kept)]
        rows, w_vm, out_vm, row_sems, w_sems, out_sems = refs[-6:]
        put, fetch, send = [], [], []
        for i, (r, d) in enumerate(sides(n_u)):
            src, share = (ins[i], share_at(r, d, n_u)) if apart else (ins[0].at[i], i)
            cols = pl.ds(pl.multiple_of(share * DH, DH), DH)
            put.append(pltpu.make_async_copy(src, rows.at[:, cols], row_sems.at[i]))
        for t in range(n_tiles):
            for k in range(n_chunks):
                cols = pl.ds(t * tile, tile)
                src = w_ref.at[pl.ds(slot * depth + k * chunk, chunk), cols]
                dst = w_vm.at[pl.ds(k * chunk, chunk), cols]
                fetch.append(pltpu.make_async_copy(src, dst, w_sems.at[t, k]))
        for c in put + fetch:
            c.start()
        for c in put:
            c.wait()
        for t in range(n_tiles):
            cols = pl.ds(t * tile, tile)
            for c in fetch[t * n_chunks : (t + 1) * n_chunks]:
                c.wait()
            total = jnp.dot(rows[...], w_vm[:, cols], preferred_element_type=jnp.float32)
            if kept:
                total = total + refs[n_in + 1][:, cols]
            if last:
                out_vm[:, cols] = total.astype(jnp.bfloat16)
                send.append(
                    pltpu.make_async_copy(out_vm.at[:, cols], out_ref.at[:, cols], out_sems.at[t])
                )
                send[-1].start()
            else:
                out_ref[:, cols] = total
        for c in send:
            c.wait()

    return pl.pallas_call(
        body,
        out_shape=jax.ShapeDtypeStruct((T, width), jnp.bfloat16 if last else jnp.float32),
        in_specs=[ANY] * (n_in + 1) + [VMEM] * len(kept),
        out_specs=ANY if last else VMEM,
        scratch_shapes=[
            pltpu.VMEM((T, depth), jnp.bfloat16),
            pltpu.VMEM((depth, width), weight.dtype),
            pltpu.VMEM((T, width if last else DH), jnp.bfloat16),
            pltpu.SemaphoreType.DMA((shares,)),
            pltpu.SemaphoreType.DMA((n_tiles, n_chunks)),
            pltpu.SemaphoreType.DMA((n_tiles,)),
        ],
        compiler_params=beside(4 * T * width + 10 * MIB),
        cost_estimate=cost(7),
        name="project",
    )(*arrays, weight, *kept)


def key_table(rand_blocks, chip, here, n_u, per):
    total = rand_blocks.shape[0]
    z = jnp.arange(n_u, dtype=jnp.int32)[:, None, None]
    core = jnp.arange(2, dtype=jnp.int32)[None, :, None]
    j = jnp.arange(per, dtype=jnp.int32)[None, None, :]
    mine = (((2 * chip + core) * n_u + z) * per + j).reshape(-1)
    window = jnp.stack([(mine - 1) % total, mine, (mine + 1) % total], axis=1)
    leading = jnp.broadcast_to(jnp.arange(GLOB, dtype=jnp.int32)[None, :], (mine.shape[0], GLOB))
    listed = jnp.concatenate([window, leading, rand_blocks[mine]], axis=1)
    device, inner = listed // per, listed % per
    zs, cs = device % n_u, device // n_u
    return ((((cs // 2) ^ chip) * n_u + (zs - here) % n_u) * 2 + cs % 2) * per + inner


def shards(queries, keys, values, rand_blocks, out_weight):
    n_c, n_u = lax.axis_size("ctx"), lax.axis_size("ulys")
    T, lanes = queries.shape
    hp = lanes // DH // (2 * n_u)
    c, z = lax.axis_index("ctx"), lax.axis_index("ulys")
    table = key_table(rand_blocks, c // 2, z, n_u, T // BLK)

    bundles = [[(1, h + 1), (2, h + 1), (0, h)] for h in range(hp - 1)] + [[(0, hp - 1)]]
    *parts, mine, others = pack_first([keys, values], n_u, hp)
    along = [lax.ppermute(x, "ulys", [(i, (i + d) % n_u) for i in range(n_u)]) for d, x in enumerate(parts, 1)]
    joined = join(mine, swap_core(others, n_c), hp)
    packed = pack_rest([queries, keys, values], bundles, n_u, joined)
    near, rounds = gather_whole(joined, n_c)
    blocks = [*along, swap_core(for_other(along), n_c)]
    q_of, far, after = [], [], [table]
    for h in range(hp):
        if h == 0:
            first, second = stage(blocks, None, n_u, after)
            ready = release(packed[0], [*along, *rounds])
        else:
            first, second, ready = stage([here], packed[h], n_u, after)
        here = to_shares(ready, n_c, n_u)
        q_of.append((here, len(bundles[h]) - 1))
        far.append(gather_chips(first, second, n_c))
        after = [x for side in far[-1] for x in side[1:]]

    total = None
    for h in range(hp):
        last = h == hp - 1
        parts = attend(table, *q_of[h], h, near, far[h], n_u, last)
        parts = send_all(parts, n_c, n_u, -1) if last else to_shares(parts[0], n_c, n_u)
        total = project(parts, out_weight, h, n_u, hp, total)
    return total


def solution(mesh):
    return jax.shard_map(
        shards,
        mesh=mesh,
        in_specs=(
            P(("ctx", "ulys"), None),
            P(("ctx", "ulys"), None),
            P(("ctx", "ulys"), None),
            P(),
            P(),
        ),
        out_specs=P(("ctx", "ulys"), None),
        check_vma=False,
    )
```

```python
import functools

import jax
import jax.numpy as jnp
from jax import lax
from jax.experimental import pallas as pl
from jax.experimental.pallas import tpu as pltpu
from jax.sharding import PartitionSpec as P

DH = 128
BLK = 64
GLOB = 2
RAND = 3
MIB = 1 << 20
LOG2E = 1.4426950408889634

ANY = pl.BlockSpec(memory_space=pl.ANY)
VMEM = pl.BlockSpec(memory_space=pltpu.VMEM)


WHOLE = pltpu.CompilerParams(vmem_limit_bytes=60 * MIB)


def beside(n_bytes):
    return pltpu.CompilerParams(vmem_limit_bytes=60 * MIB - n_bytes)


def cost(us):
    return pl.CostEstimate(flops=us * 1_150_000_000, bytes_accessed=0, transcendentals=0)


def copy_all(pairs, sems):
    copies = [pltpu.make_async_copy(src, dst, sems.at[i]) for i, (src, dst) in enumerate(pairs)]
    for c in copies:
        c.start()
    for c in copies:
        c.wait()


def sides(n_u):
    return [(r, d) for d in range(n_u) for r in range(2)]


def share_at(r, d, n_u):
    z, core = lax.axis_index("ulys"), lax.rem(lax.axis_index("ctx"), 2)
    return 2 * lax.rem(z + d + n_u, n_u) + (core if r == 0 else 1 - core)


def pack_first(tensors, n_u, hp):
    T, nb, n_s = tensors[0].shape[0], len(tensors), 2 * n_u

    def body(*refs):
        ins, outs = refs[:nb], refs[nb : nb + n_u + 1]
        held, near, in_sems, out_sems = refs[nb + n_u + 1 :]
        z, core = lax.axis_index("ulys"), lax.rem(lax.axis_index("ctx"), 2)
        pairs = [(ins[i].at[:, pl.ds(0, n_s * DH)], held.at[i]) for i in range(nb)]
        for h in range(hp):
            cols = pl.ds(pl.multiple_of((h * n_s + 2 * z) * DH, DH), 2 * DH)
            pairs += [(ins[i].at[:, cols], near.at[h * nb + i]) for i in range(nb)]
        copy_all(pairs, in_sems)
        pairs = []
        for r in range(2):
            for d in range(1, n_u):
                cols = pl.ds(pl.multiple_of(share_at(r, d, n_u) * DH, DH), DH)
                pairs += [(held.at[i, :, cols], outs[d - 1].at[r, i]) for i in range(nb)]
            cols = pl.ds(pl.multiple_of((core if r == 0 else 1 - core) * DH, DH), DH)
            pairs += [(near.at[i, :, cols], outs[n_u - 1 + r].at[i]) for i in range(hp * nb)]
        copy_all(pairs, out_sems)

    shapes = [(2, nb, T, DH)] * (n_u - 1) + [(hp * nb, T, DH)] * 2
    return pl.pallas_call(
        body,
        out_shape=[jax.ShapeDtypeStruct(x, jnp.bfloat16) for x in shapes],
        in_specs=[ANY] * nb,
        out_specs=[ANY] * (n_u + 1),
        scratch_shapes=[
            pltpu.VMEM((nb, T, n_s * DH), jnp.bfloat16),
            pltpu.VMEM((hp * nb, T, 2 * DH), jnp.bfloat16),
            pltpu.SemaphoreType.DMA(((1 + hp) * nb,)),
            pltpu.SemaphoreType.DMA(((n_s - 2 + 2 * hp) * nb,)),
        ],
        compiler_params=beside(8 * MIB),
        cost_estimate=cost(2),
        name="pack_first",
    )(*tensors)


def for_other(parts):
    n = len(parts)

    def body(*refs):
        copy_all([(refs[i].at[1], refs[n].at[i]) for i in range(n)], refs[n + 1])

    return pl.pallas_call(
        body,
        out_shape=jax.ShapeDtypeStruct((n, *parts[0].shape[1:]), jnp.bfloat16),
        in_specs=[ANY] * n,
        out_specs=VMEM,
        scratch_shapes=[pltpu.SemaphoreType.DMA((n,))],
        compiler_params=beside(8 * MIB),
        cost_estimate=cost(4),
        name="for_other",
    )(*parts)


def release(packed, after):
    def body(*refs):
        pass

    return pl.pallas_call(
        body,
        out_shape=jax.ShapeDtypeStruct(packed.shape, packed.dtype),
        in_specs=[ANY] * (1 + len(after)),
        out_specs=ANY,
        input_output_aliases={0: 0},
        compiler_params=beside(8 * MIB),
        cost_estimate=cost(1),
        name="release",
    )(packed, *after)


def join(mine, other, hp):
    n, T, _ = mine.shape
    nb = n // hp

    def body(mine_ref, other_ref, out, sems):
        core = lax.rem(lax.axis_index("ctx"), 2)
        pairs = []
        for r, ref in enumerate((mine_ref, other_ref)):
            for h in range(hp):
                for i in range(nb):
                    at = (2 * (i * hp + h) + (core if r == 0 else 1 - core)) * T
                    pairs.append((ref.at[h * nb + i], out.at[pl.ds(pl.multiple_of(at, T), T)]))
        copy_all(pairs, sems)

    return pl.pallas_call(
        body,
        out_shape=jax.ShapeDtypeStruct((2 * n * T, DH), jnp.bfloat16),
        in_specs=[ANY] * 2,
        out_specs=VMEM,
        scratch_shapes=[pltpu.SemaphoreType.DMA((2 * hp * nb,))],
        compiler_params=beside(8 * MIB),
        cost_estimate=cost(2),
        name="join",
    )(mine, other)


def pack_rest(tensors, bundles, n_u, after):
    T, nb, n_s = tensors[0].shape[0], len(tensors), 2 * n_u
    items = [item for bundle in bundles for item in bundle]

    def body(*refs):
        ins, outs = refs[:nb], refs[nb + 1 : nb + 1 + len(bundles)]
        held, in_sems, out_sems = refs[nb + 1 + len(bundles) :]
        pairs, where = [], [(b, i) for b, bundle in enumerate(bundles) for i in range(len(bundle))]
        for n, (which, slot) in enumerate(items):
            pairs.append((ins[which].at[:, pl.ds(slot * n_s * DH, n_s * DH)], held.at[n]))
        copy_all(pairs, in_sems)
        pairs = []
        for n, (b, i) in enumerate(where):
            for k in range(n_s):
                pairs.append((held.at[n, :, pl.ds(k * DH, DH)], outs[b].at[k, i]))
        copy_all(pairs, out_sems)

    return pl.pallas_call(
        body,
        out_shape=[jax.ShapeDtypeStruct((n_s, len(b), T, DH), jnp.bfloat16) for b in bundles],
        in_specs=[ANY] * (nb + 1),
        out_specs=[ANY] * len(bundles),
        scratch_shapes=[
            pltpu.VMEM((len(items), T, n_s * DH), jnp.bfloat16),
            pltpu.SemaphoreType.DMA((len(items),)),
            pltpu.SemaphoreType.DMA((len(items) * n_s,)),
        ],
        compiler_params=beside(8 * MIB),
        cost_estimate=cost(3),
        name="pack_rest",
    )(*tensors, after)


def stage(blocks, packed, n_u, after):
    n_s, n_b, T = 2 * n_u, len(blocks), blocks[0].shape[2]
    last = [] if packed is None else [packed]
    n_in = n_b + len(last) + len(after)

    def body(*refs):
        z, core = lax.axis_index("ulys"), lax.rem(lax.axis_index("ctx"), 2)
        outs, sems = refs[n_in : n_in + 2], refs[-1]
        pairs = []
        for k in range(2, n_s):
            d, c = k // 2, k % 2
            if n_b == 1:
                block, at = refs[0].at[2 * lax.rem(z + d, n_u) + c], (k - 2) * T
            else:
                block = refs[n_u - d - 1].at[0] if c == 0 else refs[n_b - 1].at[n_u - d - 1]
                at = (2 * (d - 1) + (core if c == 0 else 1 - core)) * T
            pairs += [(block.at[i], outs[i].at[pl.ds(pl.multiple_of(at, T), T)]) for i in range(2)]
        copy_all(pairs, sems)

    shapes = [((n_s - 2) * T, DH)] * 2 + [x.shape for x in last]
    return pl.pallas_call(
        body,
        out_shape=[jax.ShapeDtypeStruct(x, jnp.bfloat16) for x in shapes],
        in_specs=[ANY] * n_in,
        out_specs=[VMEM] * 2 + [ANY] * len(last),
        input_output_aliases={n_b: 2} if last else {},
        scratch_shapes=[pltpu.SemaphoreType.DMA((2 * (n_s - 2),))],
        compiler_params=beside(8 * MIB),
        cost_estimate=cost(3),
        name="stage",
    )(*blocks, *last, *after)


def to_shares(x, n_c, n_u):
    groups = [
        [(2 * p + core) * n_u + z for z in range(n_u) for core in range(2)] for p in range(n_c // 2)
    ]
    return lax.all_to_all(
        x, ("ctx", "ulys"), split_axis=0, concat_axis=0, tiled=True, axis_index_groups=groups
    )


def send(x, r, d, n_c, n_u):
    if (r, d) == (0, 0):
        return x
    pairs = [(c * n_u + z, (c ^ r) * n_u + (z + d) % n_u) for c in range(n_c) for z in range(n_u)]
    return lax.ppermute(x, ("ctx", "ulys"), pairs)


def send_all(parts, n_c, n_u, sign):
    return [send(x, r, (sign * d) % n_u, n_c, n_u) for x, (r, d) in zip(parts, sides(n_u))]


def swap_core(x, n_c):
    return lax.ppermute(x, "ctx", [(i, i ^ 1) for i in range(n_c)])


def swap_chip(x, bit, n_c):
    return lax.ppermute(x, "ctx", [(i, i ^ (2 * bit)) for i in range(n_c)])


def gather_whole(x, n_c):
    n_p, half = n_c // 2, x.shape[0] // 2
    got, halves = [], {0: [(x, 0), (x, half)]}

    def again(part, bit):
        y, at = part
        got.append(swap_chip(y if y.shape[0] == half else y[at : at + half], bit, n_c))
        return (got[-1], 0)

    for t in range(1, n_p):
        if t & (t - 1) == 0:
            got.append(swap_chip(x, t, n_c))
            halves[t] = [(got[-1], 0), (got[-1], half)]
    for t in range(1, n_p):
        if t & (t - 1) != 0:
            low, high = t & -t, 1 << (t.bit_length() - 1)
            halves[t] = [again(halves[t ^ low][0], low), again(halves[t ^ high][1], high)]
    return [[halves[t][i] for t in range(n_p)] for i in range(2)], got


def gather_chips(first, second, n_c):
    n_p = n_c // 2
    bits = [1 << i for i in range(n_p.bit_length() - 1)]
    a, b = {0: first}, {0: second}
    for t in reversed(bits):
        a[t] = swap_chip(first, t, n_c)
    for t in bits:
        b[t] = swap_chip(second, t, n_c)
    for t in range(1, n_p):
        if t not in bits:
            low, high = t & -t, 1 << (t.bit_length() - 1)
            a[t] = swap_chip(a[t ^ low], low, n_c)
            b[t] = swap_chip(b[t ^ high], high, n_c)
    return [a[t] for t in range(n_p)], [b[t] for t in range(n_p)]


def attend(table, queries, q_index, slot, near, far, n_u, apart):
    n_s, _, T, _ = queries.shape
    n_q = n_s * T
    span = n_s * T
    n_k = span * len(far[0])
    parts = []
    for nears, fars in zip(near, far):
        for t, ((x, at), y) in enumerate(zip(nears, fars)):
            parts.append((x, at + slot * 2 * T, t * span, 2 * T))
            parts.append((y, 0, t * span + 2 * T, span - 2 * T))
    n_half = len(parts) // 2
    n_rows, n_list = table.shape
    group = 4 * T // BLK
    arrays = [queries, *(x for x, _, _, _ in parts)]
    n_in, n_out = len(arrays), 2 * n_u if apart else 1

    def body(table_ref, *refs):
        ins, outs = refs[:n_in], refs[n_in : n_in + n_out]
        table, q_vm, k_vm, v_vm, o_vm, sems, out_sems = refs[n_in + n_out :]
        pairs = [(table_ref, table)]
        for k in range(n_s):
            pairs.append((ins[0].at[k, q_index], q_vm.at[pl.ds(k * T, T)]))
        for i, (ref, (_, src, dst, n)) in enumerate(zip(ins[1:], parts)):
            vm = k_vm if i < n_half else v_vm
            pairs.append((ref.at[pl.ds(src, n)], vm.at[pl.ds(dst, n)]))
        copies = [pltpu.make_async_copy(a, b, sems.at[i]) for i, (a, b) in enumerate(pairs)]
        for c in copies:
            c.start()
        for c in copies[: 1 + n_s + n_half]:
            c.wait()
        for step in range(n_rows // group):
            rows = range(step * group, (step + 1) * group)
            at = [[pl.multiple_of(table[r, j] * BLK, BLK) for j in range(n_list)] for r in rows]
            s = []
            for r, listed in zip(rows, at):
                k = jnp.concatenate([k_vm[pl.ds(a, BLK), :] for a in listed], axis=0)
                s.append(
                    lax.dot_general(
                        q_vm[pl.ds(r * BLK, BLK), :],
                        k,
                        (((1,), (1,)), ((), ())),
                        preferred_element_type=jnp.float32,
                    )
                )
            s = jnp.concatenate(s, axis=0)
            e = jnp.exp2((s - jnp.max(s, axis=-1, keepdims=True)) * (DH**-0.5 * LOG2E))
            w = (e * (1.0 / jnp.sum(e, axis=-1, keepdims=True))).astype(jnp.bfloat16)
            if step == 0:
                for c in copies[1 + n_s + n_half :]:
                    c.wait()
            for g, (r, listed) in enumerate(zip(rows, at)):
                v = jnp.concatenate([v_vm[pl.ds(a, BLK), :] for a in listed], axis=0)
                o = jnp.dot(
                    w[g * BLK : (g + 1) * BLK], v, preferred_element_type=jnp.float32
                )
                o_vm[pl.ds(r * BLK, BLK), :] = o.astype(jnp.bfloat16)

        pairs = []
        if apart:
            for out, (r, d) in zip(outs, sides(n_u)):
                at = pl.multiple_of(share_at(r, -d, n_u) * T, T)
                pairs.append((o_vm.at[pl.ds(at, T)], out))
        else:
            for k in range(n_s):
                pairs.append((o_vm.at[pl.ds(k * T, T)], outs[0].at[k]))
        copy_all(pairs, out_sems)

    return pl.pallas_call(
        body,
        out_shape=[jax.ShapeDtypeStruct((T, DH) if apart else (n_s, T, DH), jnp.bfloat16)] * n_out,
        in_specs=[ANY] * (1 + n_in),
        out_specs=[ANY] * n_out,
        scratch_shapes=[
            pltpu.SMEM(table.shape, jnp.int32),
            pltpu.VMEM((n_q, DH), jnp.bfloat16),
            pltpu.VMEM((n_k, DH), jnp.bfloat16),
            pltpu.VMEM((n_k, DH), jnp.bfloat16),
            pltpu.VMEM((n_q, DH), jnp.bfloat16),
            pltpu.SemaphoreType.DMA((n_s + n_in,)),
            pltpu.SemaphoreType.DMA((n_s,)),
        ],
        compiler_params=WHOLE,
        cost_estimate=cost(8),
        name="attend",
    )(table, *arrays)


def project(parts, weight, slot, n_u, hp, partial):
    apart, last = isinstance(parts, list), slot == hp - 1
    arrays = parts if apart else [parts]
    T = arrays[0].shape[-2]
    width = weight.shape[1]
    shares = 2 * n_u
    depth = shares * DH
    n_tiles, n_chunks = 2, 1
    tile, chunk = width // n_tiles, depth // n_chunks
    n_in = len(arrays)
    kept = [] if partial is None else [partial]

    def body(*refs):
        ins, w_ref, out_ref = refs[:n_in], refs[n_in], refs[n_in + 1 + len(kept)]
        rows, w_vm, out_vm, row_sems, w_sems, out_sems = refs[-6:]
        put, fetch, send = [], [], []
        for i, (r, d) in enumerate(sides(n_u)):
            src, share = (ins[i], share_at(r, d, n_u)) if apart else (ins[0].at[i], i)
            cols = pl.ds(pl.multiple_of(share * DH, DH), DH)
            put.append(pltpu.make_async_copy(src, rows.at[:, cols], row_sems.at[i]))
        for t in range(n_tiles):
            for k in range(n_chunks):
                cols = pl.ds(t * tile, tile)
                src = w_ref.at[pl.ds(slot * depth + k * chunk, chunk), cols]
                dst = w_vm.at[pl.ds(k * chunk, chunk), cols]
                fetch.append(pltpu.make_async_copy(src, dst, w_sems.at[t, k]))
        for c in put + fetch:
            c.start()
        for c in put:
            c.wait()
        for t in range(n_tiles):
            cols = pl.ds(t * tile, tile)
            for c in fetch[t * n_chunks : (t + 1) * n_chunks]:
                c.wait()
            total = jnp.dot(rows[...], w_vm[:, cols], preferred_element_type=jnp.float32)
            if kept:
                total = total + refs[n_in + 1][:, cols]
            if last:
                out_vm[:, cols] = total.astype(jnp.bfloat16)
                send.append(
                    pltpu.make_async_copy(out_vm.at[:, cols], out_ref.at[:, cols], out_sems.at[t])
                )
                send[-1].start()
            else:
                out_ref[:, cols] = total
        for c in send:
            c.wait()

    return pl.pallas_call(
        body,
        out_shape=jax.ShapeDtypeStruct((T, width), jnp.bfloat16 if last else jnp.float32),
        in_specs=[ANY] * (n_in + 1) + [VMEM] * len(kept),
        out_specs=ANY if last else VMEM,
        scratch_shapes=[
            pltpu.VMEM((T, depth), jnp.bfloat16),
            pltpu.VMEM((depth, width), weight.dtype),
            pltpu.VMEM((T, width if last else DH), jnp.bfloat16),
            pltpu.SemaphoreType.DMA((shares,)),
            pltpu.SemaphoreType.DMA((n_tiles, n_chunks)),
            pltpu.SemaphoreType.DMA((n_tiles,)),
        ],
        compiler_params=beside(4 * T * width + 10 * MIB),
        cost_estimate=cost(7),
        name="project",
    )(*arrays, weight, *kept)


def key_table(rand_blocks, chip, here, n_u, per):
    total = rand_blocks.shape[0]
    z = jnp.arange(n_u, dtype=jnp.int32)[:, None, None]
    core = jnp.arange(2, dtype=jnp.int32)[None, :, None]
    j = jnp.arange(per, dtype=jnp.int32)[None, None, :]
    mine = (((2 * chip + core) * n_u + z) * per + j).reshape(-1)
    window = jnp.stack([(mine - 1) % total, mine, (mine + 1) % total], axis=1)
    leading = jnp.broadcast_to(jnp.arange(GLOB, dtype=jnp.int32)[None, :], (mine.shape[0], GLOB))
    listed = jnp.concatenate([window, leading, rand_blocks[mine]], axis=1)
    device, inner = listed // per, listed % per
    zs, cs = device % n_u, device // n_u
    return ((((cs // 2) ^ chip) * n_u + (zs - here) % n_u) * 2 + cs % 2) * per + inner


def shards(queries, keys, values, rand_blocks, out_weight):
    n_c, n_u = lax.axis_size("ctx"), lax.axis_size("ulys")
    T, lanes = queries.shape
    hp = lanes // DH // (2 * n_u)
    c, z = lax.axis_index("ctx"), lax.axis_index("ulys")
    table = key_table(rand_blocks, c // 2, z, n_u, T // BLK)

    bundles = [[(1, h + 1), (2, h + 1), (0, h)] for h in range(hp - 1)] + [[(0, hp - 1)]]
    *parts, mine, others = pack_first([keys, values], n_u, hp)
    along = [lax.ppermute(x, "ulys", [(i, (i + d) % n_u) for i in range(n_u)]) for d, x in enumerate(parts, 1)]
    joined = join(mine, swap_core(others, n_c), hp)
    packed = pack_rest([queries, keys, values], bundles, n_u, joined)
    near, rounds = gather_whole(joined, n_c)
    meant = for_other(along)
    blocks = [*along, swap_core(meant, n_c)]
    q_of, far, after = [], [], [table]
    direct = (n_c // 2).bit_length() - 1
    for h in range(hp):
        if h == 0:
            first, second = stage(blocks, None, n_u, after)
            ready = release(packed[0], [meant, *rounds[:direct]])
        else:
            first, second, ready = stage([here], packed[h], n_u, after)
        here = to_shares(ready, n_c, n_u)
        q_of.append((here, len(bundles[h]) - 1))
        far.append(gather_chips(first, second, n_c))
        after = [x for side in far[-1] for x in side[1:]] + rounds[direct:]
        rounds = rounds[:direct]

    total = None
    for h in range(hp):
        last = h == hp - 1
        parts = attend(table, *q_of[h], h, near, far[h], n_u, last)
        parts = send_all(parts, n_c, n_u, -1) if last else to_shares(parts[0], n_c, n_u)
        total = project(parts, out_weight, h, n_u, hp, total)
    return total


def solution(mesh):
    return jax.shard_map(
        shards,
        mesh=mesh,
        in_specs=(
            P(("ctx", "ulys"), None),
            P(("ctx", "ulys"), None),
            P(("ctx", "ulys"), None),
            P(),
            P(),
        ),
        out_specs=P(("ctx", "ulys"), None),
        check_vma=False,
    )
```

```python
import functools

import jax
import jax.numpy as jnp
from jax import lax
from jax.experimental import pallas as pl
from jax.experimental.pallas import tpu as pltpu
from jax.sharding import PartitionSpec as P

DH = 128
BLK = 64
GLOB = 2
RAND = 3
MIB = 1 << 20
LOG2E = 1.4426950408889634

ANY = pl.BlockSpec(memory_space=pl.ANY)
VMEM = pl.BlockSpec(memory_space=pltpu.VMEM)


WHOLE = pltpu.CompilerParams(vmem_limit_bytes=60 * MIB)


def beside(n_bytes):
    return pltpu.CompilerParams(vmem_limit_bytes=60 * MIB - n_bytes)


def cost(us):
    return pl.CostEstimate(flops=us * 1_150_000_000, bytes_accessed=0, transcendentals=0)


def copy_all(pairs, sems):
    copies = [pltpu.make_async_copy(src, dst, sems.at[i]) for i, (src, dst) in enumerate(pairs)]
    for c in copies:
        c.start()
    for c in copies:
        c.wait()


def sides(n_u):
    return [(r, d) for d in range(n_u) for r in range(2)]


def share_at(r, d, n_u):
    z, core = lax.axis_index("ulys"), lax.rem(lax.axis_index("ctx"), 2)
    return 2 * lax.rem(z + d + n_u, n_u) + (core if r == 0 else 1 - core)


def pack_first(tensors, n_u, hp):
    T, nb, n_s = tensors[0].shape[0], len(tensors), 2 * n_u

    def body(*refs):
        ins, outs = refs[:nb], refs[nb : nb + n_u + 1]
        held, near, in_sems, out_sems = refs[nb + n_u + 1 :]
        z, core = lax.axis_index("ulys"), lax.rem(lax.axis_index("ctx"), 2)
        pairs = [(ins[i].at[:, pl.ds(0, n_s * DH)], held.at[i]) for i in range(nb)]
        for h in range(hp):
            cols = pl.ds(pl.multiple_of((h * n_s + 2 * z) * DH, DH), 2 * DH)
            pairs += [(ins[i].at[:, cols], near.at[h * nb + i]) for i in range(nb)]
        copy_all(pairs, in_sems)
        pairs = []
        for r in range(2):
            for d in range(1, n_u):
                cols = pl.ds(pl.multiple_of(share_at(r, d, n_u) * DH, DH), DH)
                pairs += [(held.at[i, :, cols], outs[d - 1].at[r, i]) for i in range(nb)]
            cols = pl.ds(pl.multiple_of((core if r == 0 else 1 - core) * DH, DH), DH)
            pairs += [(near.at[i, :, cols], outs[n_u - 1 + r].at[i]) for i in range(hp * nb)]
        copy_all(pairs, out_sems)

    shapes = [(2, nb, T, DH)] * (n_u - 1) + [(hp * nb, T, DH)] * 2
    return pl.pallas_call(
        body,
        out_shape=[jax.ShapeDtypeStruct(x, jnp.bfloat16) for x in shapes],
        in_specs=[ANY] * nb,
        out_specs=[ANY] * (n_u + 1),
        scratch_shapes=[
            pltpu.VMEM((nb, T, n_s * DH), jnp.bfloat16),
            pltpu.VMEM((hp * nb, T, 2 * DH), jnp.bfloat16),
            pltpu.SemaphoreType.DMA(((1 + hp) * nb,)),
            pltpu.SemaphoreType.DMA(((n_s - 2 + 2 * hp) * nb,)),
        ],
        compiler_params=beside(8 * MIB),
        cost_estimate=cost(2),
        name="pack_first",
    )(*tensors)


def for_other(parts):
    n = len(parts)

    def body(*refs):
        copy_all([(refs[i].at[1], refs[n].at[i]) for i in range(n)], refs[n + 1])

    return pl.pallas_call(
        body,
        out_shape=jax.ShapeDtypeStruct((n, *parts[0].shape[1:]), jnp.bfloat16),
        in_specs=[ANY] * n,
        out_specs=VMEM,
        scratch_shapes=[pltpu.SemaphoreType.DMA((n,))],
        compiler_params=beside(8 * MIB),
        cost_estimate=cost(4),
        name="for_other",
    )(*parts)


def release(packed, after):
    def body(*refs):
        pass

    return pl.pallas_call(
        body,
        out_shape=jax.ShapeDtypeStruct(packed.shape, packed.dtype),
        in_specs=[ANY] * (1 + len(after)),
        out_specs=ANY,
        input_output_aliases={0: 0},
        compiler_params=beside(8 * MIB),
        cost_estimate=cost(1),
        name="release",
    )(packed, *after)


def join(mine, other, hp):
    n, T, _ = mine.shape
    nb = n // hp

    def body(mine_ref, other_ref, out, sems):
        core = lax.rem(lax.axis_index("ctx"), 2)
        pairs = []
        for r, ref in enumerate((mine_ref, other_ref)):
            for h in range(hp):
                for i in range(nb):
                    at = (2 * (i * hp + h) + (core if r == 0 else 1 - core)) * T
                    pairs.append((ref.at[h * nb + i], out.at[pl.ds(pl.multiple_of(at, T), T)]))
        copy_all(pairs, sems)

    return pl.pallas_call(
        body,
        out_shape=jax.ShapeDtypeStruct((2 * n * T, DH), jnp.bfloat16),
        in_specs=[ANY] * 2,
        out_specs=VMEM,
        scratch_shapes=[pltpu.SemaphoreType.DMA((2 * hp * nb,))],
        compiler_params=beside(8 * MIB),
        cost_estimate=cost(2),
        name="join",
    )(mine, other)


def pack_rest(tensors, bundles, n_u, after):
    T, nb, n_s = tensors[0].shape[0], len(tensors), 2 * n_u
    items = [item for bundle in bundles for item in bundle]

    def body(*refs):
        ins, outs = refs[:nb], refs[nb + len(after) : nb + len(after) + len(bundles)]
        held, in_sems, out_sems = refs[nb + len(after) + len(bundles) :]
        pairs, where = [], [(b, i) for b, bundle in enumerate(bundles) for i in range(len(bundle))]
        for n, (which, slot) in enumerate(items):
            pairs.append((ins[which].at[:, pl.ds(slot * n_s * DH, n_s * DH)], held.at[n]))
        copy_all(pairs, in_sems)
        pairs = []
        for n, (b, i) in enumerate(where):
            for k in range(n_s):
                pairs.append((held.at[n, :, pl.ds(k * DH, DH)], outs[b].at[k, i]))
        copy_all(pairs, out_sems)

    return pl.pallas_call(
        body,
        out_shape=[jax.ShapeDtypeStruct((n_s, len(b), T, DH), jnp.bfloat16) for b in bundles],
        in_specs=[ANY] * (nb + len(after)),
        out_specs=[ANY] * len(bundles),
        scratch_shapes=[
            pltpu.VMEM((len(items), T, n_s * DH), jnp.bfloat16),
            pltpu.SemaphoreType.DMA((len(items),)),
            pltpu.SemaphoreType.DMA((len(items) * n_s,)),
        ],
        compiler_params=beside(8 * MIB),
        cost_estimate=cost(3),
        name="pack_rest",
    )(*tensors, *after)


def stage(blocks, packed, n_u, after):
    n_s, n_b, T = 2 * n_u, len(blocks), blocks[0].shape[2]
    last = [] if packed is None else [packed]
    n_in = n_b + len(last) + len(after)

    def body(*refs):
        z, core = lax.axis_index("ulys"), lax.rem(lax.axis_index("ctx"), 2)
        outs, sems = refs[n_in : n_in + 2], refs[-1]
        pairs = []
        for k in range(2, n_s):
            d, c = k // 2, k % 2
            if n_b == 1:
                block, at = refs[0].at[2 * lax.rem(z + d, n_u) + c], (k - 2) * T
            else:
                block = refs[n_u - d - 1].at[0] if c == 0 else refs[n_b - 1].at[n_u - d - 1]
                at = (2 * (d - 1) + (core if c == 0 else 1 - core)) * T
            pairs += [(block.at[i], outs[i].at[pl.ds(pl.multiple_of(at, T), T)]) for i in range(2)]
        copy_all(pairs, sems)

    shapes = [((n_s - 2) * T, DH)] * 2 + [x.shape for x in last]
    return pl.pallas_call(
        body,
        out_shape=[jax.ShapeDtypeStruct(x, jnp.bfloat16) for x in shapes],
        in_specs=[ANY] * n_in,
        out_specs=[VMEM] * 2 + [ANY] * len(last),
        input_output_aliases={n_b: 2} if last else {},
        scratch_shapes=[pltpu.SemaphoreType.DMA((2 * (n_s - 2),))],
        compiler_params=beside(8 * MIB),
        cost_estimate=cost(3),
        name="stage",
    )(*blocks, *last, *after)


def to_shares(x, n_c, n_u):
    groups = [
        [(2 * p + core) * n_u + z for z in range(n_u) for core in range(2)] for p in range(n_c // 2)
    ]
    return lax.all_to_all(
        x, ("ctx", "ulys"), split_axis=0, concat_axis=0, tiled=True, axis_index_groups=groups
    )


def send(x, r, d, n_c, n_u):
    if (r, d) == (0, 0):
        return x
    pairs = [(c * n_u + z, (c ^ r) * n_u + (z + d) % n_u) for c in range(n_c) for z in range(n_u)]
    return lax.ppermute(x, ("ctx", "ulys"), pairs)


def send_all(parts, n_c, n_u, sign):
    return [send(x, r, (sign * d) % n_u, n_c, n_u) for x, (r, d) in zip(parts, sides(n_u))]


def swap_core(x, n_c):
    return lax.ppermute(x, "ctx", [(i, i ^ 1) for i in range(n_c)])


def swap_chip(x, bit, n_c):
    return lax.ppermute(x, "ctx", [(i, i ^ (2 * bit)) for i in range(n_c)])


def gather_whole(x, n_c):
    n_p, half = n_c // 2, x.shape[0] // 2
    got, halves = [], {0: [(x, 0), (x, half)]}

    def again(part, bit):
        y, at = part
        got.append(swap_chip(y if y.shape[0] == half else y[at : at + half], bit, n_c))
        return (got[-1], 0)

    for t in range(1, n_p):
        if t & (t - 1) == 0:
            got.append(swap_chip(x, t, n_c))
            halves[t] = [(got[-1], 0), (got[-1], half)]
    for t in range(1, n_p):
        if t & (t - 1) != 0:
            low, high = t & -t, 1 << (t.bit_length() - 1)
            halves[t] = [again(halves[t ^ low][0], low), again(halves[t ^ high][1], high)]
    return [[halves[t][i] for t in range(n_p)] for i in range(2)], got


def gather_chips(first, second, n_c):
    n_p = n_c // 2
    bits = [1 << i for i in range(n_p.bit_length() - 1)]
    a, b = {0: first}, {0: second}
    for t in reversed(bits):
        a[t] = swap_chip(first, t, n_c)
    for t in bits:
        b[t] = swap_chip(second, t, n_c)
    for t in range(1, n_p):
        if t not in bits:
            low, high = t & -t, 1 << (t.bit_length() - 1)
            a[t] = swap_chip(a[t ^ low], low, n_c)
            b[t] = swap_chip(b[t ^ high], high, n_c)
    return [a[t] for t in range(n_p)], [b[t] for t in range(n_p)]


def attend(table, queries, q_index, slot, near, far, n_u, apart):
    n_s, _, T, _ = queries.shape
    n_q = n_s * T
    span = n_s * T
    n_k = span * len(far[0])
    parts = []
    for nears, fars in zip(near, far):
        for t, ((x, at), y) in enumerate(zip(nears, fars)):
            parts.append((x, at + slot * 2 * T, t * span, 2 * T))
            parts.append((y, 0, t * span + 2 * T, span - 2 * T))
    n_half = len(parts) // 2
    n_rows, n_list = table.shape
    group = 4 * T // BLK
    arrays = [queries, *(x for x, _, _, _ in parts)]
    n_in, n_out = len(arrays), 2 * n_u if apart else 1

    def body(table_ref, *refs):
        ins, outs = refs[:n_in], refs[n_in : n_in + n_out]
        table, q_vm, k_vm, v_vm, o_vm, sems, out_sems = refs[n_in + n_out :]
        pairs = [(table_ref, table)]
        for k in range(n_s):
            pairs.append((ins[0].at[k, q_index], q_vm.at[pl.ds(k * T, T)]))
        for i, (ref, (_, src, dst, n)) in enumerate(zip(ins[1:], parts)):
            vm = k_vm if i < n_half else v_vm
            pairs.append((ref.at[pl.ds(src, n)], vm.at[pl.ds(dst, n)]))
        copies = [pltpu.make_async_copy(a, b, sems.at[i]) for i, (a, b) in enumerate(pairs)]
        for c in copies:
            c.start()
        for c in copies[: 1 + n_s + n_half]:
            c.wait()
        for step in range(n_rows // group):
            rows = range(step * group, (step + 1) * group)
            at = [[pl.multiple_of(table[r, j] * BLK, BLK) for j in range(n_list)] for r in rows]
            s = []
            for r, listed in zip(rows, at):
                k = jnp.concatenate([k_vm[pl.ds(a, BLK), :] for a in listed], axis=0)
                s.append(
                    lax.dot_general(
                        q_vm[pl.ds(r * BLK, BLK), :],
                        k,
                        (((1,), (1,)), ((), ())),
                        preferred_element_type=jnp.float32,
                    )
                )
            s = jnp.concatenate(s, axis=0)
            e = jnp.exp2((s - jnp.max(s, axis=-1, keepdims=True)) * (DH**-0.5 * LOG2E))
            w = (e * (1.0 / jnp.sum(e, axis=-1, keepdims=True))).astype(jnp.bfloat16)
            if step == 0:
                for c in copies[1 + n_s + n_half :]:
                    c.wait()
            for g, (r, listed) in enumerate(zip(rows, at)):
                v = jnp.concatenate([v_vm[pl.ds(a, BLK), :] for a in listed], axis=0)
                o = jnp.dot(
                    w[g * BLK : (g + 1) * BLK], v, preferred_element_type=jnp.float32
                )
                o_vm[pl.ds(r * BLK, BLK), :] = o.astype(jnp.bfloat16)

        pairs = []
        if apart:
            for out, (r, d) in zip(outs, sides(n_u)):
                at = pl.multiple_of(share_at(r, -d, n_u) * T, T)
                pairs.append((o_vm.at[pl.ds(at, T)], out))
        else:
            for k in range(n_s):
                pairs.append((o_vm.at[pl.ds(k * T, T)], outs[0].at[k]))
        copy_all(pairs, out_sems)

    return pl.pallas_call(
        body,
        out_shape=[jax.ShapeDtypeStruct((T, DH) if apart else (n_s, T, DH), jnp.bfloat16)] * n_out,
        in_specs=[ANY] * (1 + n_in),
        out_specs=[ANY] * n_out,
        scratch_shapes=[
            pltpu.SMEM(table.shape, jnp.int32),
            pltpu.VMEM((n_q, DH), jnp.bfloat16),
            pltpu.VMEM((n_k, DH), jnp.bfloat16),
            pltpu.VMEM((n_k, DH), jnp.bfloat16),
            pltpu.VMEM((n_q, DH), jnp.bfloat16),
            pltpu.SemaphoreType.DMA((n_s + n_in,)),
            pltpu.SemaphoreType.DMA((n_s,)),
        ],
        compiler_params=WHOLE,
        cost_estimate=cost(8),
        name="attend",
    )(table, *arrays)


def project(parts, weight, slot, n_u, hp, partial):
    apart, last = isinstance(parts, list), slot == hp - 1
    arrays = parts if apart else [parts]
    T = arrays[0].shape[-2]
    width = weight.shape[1]
    shares = 2 * n_u
    depth = shares * DH
    n_tiles, n_chunks = 2, 1
    tile, chunk = width // n_tiles, depth // n_chunks
    n_in = len(arrays)
    kept = [] if partial is None else [partial]

    def body(*refs):
        ins, w_ref, out_ref = refs[:n_in], refs[n_in], refs[n_in + 1 + len(kept)]
        rows, w_vm, out_vm, row_sems, w_sems, out_sems = refs[-6:]
        put, fetch, send = [], [], []
        for i, (r, d) in enumerate(sides(n_u)):
            src, share = (ins[i], share_at(r, d, n_u)) if apart else (ins[0].at[i], i)
            cols = pl.ds(pl.multiple_of(share * DH, DH), DH)
            put.append(pltpu.make_async_copy(src, rows.at[:, cols], row_sems.at[i]))
        for t in range(n_tiles):
            for k in range(n_chunks):
                cols = pl.ds(t * tile, tile)
                src = w_ref.at[pl.ds(slot * depth + k * chunk, chunk), cols]
                dst = w_vm.at[pl.ds(k * chunk, chunk), cols]
                fetch.append(pltpu.make_async_copy(src, dst, w_sems.at[t, k]))
        for c in put + fetch:
            c.start()
        for c in put:
            c.wait()
        for t in range(n_tiles):
            cols = pl.ds(t * tile, tile)
            for c in fetch[t * n_chunks : (t + 1) * n_chunks]:
                c.wait()
            total = jnp.dot(rows[...], w_vm[:, cols], preferred_element_type=jnp.float32)
            if kept:
                total = total + refs[n_in + 1][:, cols]
            if last:
                out_vm[:, cols] = total.astype(jnp.bfloat16)
                send.append(
                    pltpu.make_async_copy(out_vm.at[:, cols], out_ref.at[:, cols], out_sems.at[t])
                )
                send[-1].start()
            else:
                out_ref[:, cols] = total
        for c in send:
            c.wait()

    return pl.pallas_call(
        body,
        out_shape=jax.ShapeDtypeStruct((T, width), jnp.bfloat16 if last else jnp.float32),
        in_specs=[ANY] * (n_in + 1) + [VMEM] * len(kept),
        out_specs=ANY if last else VMEM,
        scratch_shapes=[
            pltpu.VMEM((T, depth), jnp.bfloat16),
            pltpu.VMEM((depth, width), weight.dtype),
            pltpu.VMEM((T, width if last else DH), jnp.bfloat16),
            pltpu.SemaphoreType.DMA((shares,)),
            pltpu.SemaphoreType.DMA((n_tiles, n_chunks)),
            pltpu.SemaphoreType.DMA((n_tiles,)),
        ],
        compiler_params=beside(4 * T * width + 10 * MIB),
        cost_estimate=cost(7),
        name="project",
    )(*arrays, weight, *kept)


def key_table(rand_blocks, chip, here, n_u, per):
    total = rand_blocks.shape[0]
    z = jnp.arange(n_u, dtype=jnp.int32)[:, None, None]
    core = jnp.arange(2, dtype=jnp.int32)[None, :, None]
    j = jnp.arange(per, dtype=jnp.int32)[None, None, :]
    mine = (((2 * chip + core) * n_u + z) * per + j).reshape(-1)
    window = jnp.stack([(mine - 1) % total, mine, (mine + 1) % total], axis=1)
    leading = jnp.broadcast_to(jnp.arange(GLOB, dtype=jnp.int32)[None, :], (mine.shape[0], GLOB))
    listed = jnp.concatenate([window, leading, rand_blocks[mine]], axis=1)
    device, inner = listed // per, listed % per
    zs, cs = device % n_u, device // n_u
    return ((((cs // 2) ^ chip) * n_u + (zs - here) % n_u) * 2 + cs % 2) * per + inner


def shards(queries, keys, values, rand_blocks, out_weight):
    n_c, n_u = lax.axis_size("ctx"), lax.axis_size("ulys")
    T, lanes = queries.shape
    hp = lanes // DH // (2 * n_u)
    c, z = lax.axis_index("ctx"), lax.axis_index("ulys")
    table = key_table(rand_blocks, c // 2, z, n_u, T // BLK)

    bundles = [[(1, h + 1), (2, h + 1), (0, h)] for h in range(hp - 1)] + [[(0, hp - 1)]]
    *parts, mine, others = pack_first([keys, values], n_u, hp)
    along = [lax.ppermute(x, "ulys", [(i, (i + d) % n_u) for i in range(n_u)]) for d, x in enumerate(parts, 1)]
    joined = join(mine, swap_core(others, n_c), hp)
    packed = pack_rest([queries, keys, values], bundles, n_u, [joined, table])
    near, rounds = gather_whole(joined, n_c)
    meant = for_other(along)
    blocks = [*along, swap_core(meant, n_c)]
    q_of, far, after = [], [], []
    direct = (n_c // 2).bit_length() - 1
    for h in range(hp):
        if h == 0:
            first, second = stage(blocks, None, n_u, after)
            ready = release(packed[0], [meant, *rounds[:direct]])
        else:
            first, second, ready = stage([here], packed[h], n_u, after)
        here = to_shares(ready, n_c, n_u)
        q_of.append((here, len(bundles[h]) - 1))
        far.append(gather_chips(first, second, n_c))
        after = [x for side in far[-1] for x in side[1:]] + rounds[direct:]
        rounds = rounds[:direct]

    total = None
    for h in range(hp):
        last = h == hp - 1
        parts = attend(table, *q_of[h], h, near, far[h], n_u, last)
        parts = send_all(parts, n_c, n_u, -1) if last else to_shares(parts[0], n_c, n_u)
        total = project(parts, out_weight, h, n_u, hp, total)
    return total


def solution(mesh):
    return jax.shard_map(
        shards,
        mesh=mesh,
        in_specs=(
            P(("ctx", "ulys"), None),
            P(("ctx", "ulys"), None),
            P(("ctx", "ulys"), None),
            P(),
            P(),
        ),
        out_specs=P(("ctx", "ulys"), None),
        check_vma=False,
    )
```
